256 devices in a mesh: dp: 8 (over z), pipe: 4 (over y), tensor: 8 (over x, core).
Axes of the slice: x: 4, y: 4, z: 8, core: 2. Of those that a mesh axis runs over, the one named last changes fastest.
Arguments:
- inputs: bfloat16 [256, 4, 5120], P('dp'), parts along dimension 0, may hold values from -6 to 6
- ln_gain: float32 [4, 5120], P('pipe'), may hold values from 0.1 to 1.9
- query_weight: bfloat16 [4, 5120, 3072], P('pipe', None, 'tensor'), may hold values from -0.078125 to 0.078125
- out_weight: bfloat16 [4, 3072, 5120], P('pipe', 'tensor'), may hold values from -0.15625 to 0.15625
- kv_cache: bfloat16 [4, 2, 256, 64, 3072], P('pipe', None, 'dp', None, 'tensor'), parts along dimension 2
- new_kv: bfloat16 [4, 2, 256, 4, 3072], P('pipe', None, 'dp', None, 'tensor'), parts along dimension 2, may hold values from -6 to 6
- active_heads: int32 [32, 4, 12], P('dp'), parts along dimension 0, may hold values from 0 to 23, as said below
Outputs:
- hidden_states: bfloat16 [4, 256, 4, 5120], P('pipe', 'dp', None, 'tensor'), parts along dimension 1
The draws below stay inside these ranges and needn't reach their ends.
There are 8 independent parts, one for each index of `dp`. The reference program is written for one: setup_inputs(seed, part) draws one part's arguments, and reference() takes and returns one part's arrays. A program takes and returns all parts, laid end to end along the dimension named above; an argument that names none is the same for every part. Nothing has to cross between parts.
Inputs may be any that keep to these rules, and one draw needn't show every extreme that they name: `active_heads`: each list names 12 different heads.
All inputs are finite; a program needn't handle non-finite values.
Results may differ from the reference program's by a relative error of at most 0.04.
Values may be sent and summed in bfloat16 or wider, within the bound.
No kernel may reach another device: no remote copies, remote signals or barrier semaphores. Data moves between devices by JAX's collectives and lax.ppermute only.
A program may use at most 128 MiB of HBM per device.

```python
import jax
import jax.numpy as jnp
from jax import lax

D = 5120
HEADS = 24
HEAD_DIM = 128
CACHE = 64
NEW = 4
ACTIVE = 12
MICRO = 4
MB_ROWS = 8
ROWS = 32
LAYERS = 4


def draw_kv_cache(key, part):
    key = jax.random.fold_in(key, 3)
    base = jax.random.normal(key, (LAYERS, 2, ROWS, CACHE, HEADS * HEAD_DIM), jnp.float32)
    return base.astype(jnp.bfloat16)


def draw_active_heads(key, part):
    key = jax.random.fold_in(key, 7)
    list_count = MICRO * LAYERS
    keys = jax.random.split(key, list_count)
    orders = jax.vmap(lambda single: jax.random.permutation(single, HEADS))(keys).astype(jnp.int32)
    head_ids = jnp.arange(HEADS, dtype=jnp.int32)[None, :]
    first_list = (jnp.arange(list_count, dtype=jnp.int32) == 0)[:, None]
    favoured = first_list & ((head_ids == 0) | (head_ids == HEADS - 1))
    scores = orders + jnp.where(favoured, 4 * HEADS, 0).astype(jnp.int32)
    chosen = lax.top_k(scores, ACTIVE)[1].astype(jnp.int32)
    return chosen.reshape(MICRO, LAYERS, ACTIVE)


def steps_of(key, dims, shards, smallest, top_value):
    factor_of = 1.0
    for axis_at, parts in shards:
        steps = jax.random.uniform(jax.random.fold_in(jax.random.fold_in(key, 6), axis_at), (parts,), jnp.float32, smallest / len(shards), top_value / len(shards))
        factor_of = factor_of * jnp.repeat(jnp.exp(steps), dims[axis_at] // parts).reshape((-1,) + (1,) * (len(dims) - 1 - axis_at))
    return factor_of


def scatter_about(own_key, shape, deviation, limit, cuts=(), kind=jnp.bfloat16):
    array = jax.random.normal(own_key, shape, jnp.float32) * deviation
    if len(cuts) > 0:
        array = steps_of(own_key, shape, cuts, -0.22, 0.18) * array
    return jnp.clip(array, min=-limit, max=limit).astype(kind)


def setup_inputs(seed: int = 0, part: int = 0) -> dict:
    streams_of = jax.random.split(jax.random.key(seed), 8)
    part_splits = jax.random.split(jax.random.fold_in(streams_of[7], part), 8)
    return {
        "inputs": scatter_about(part_splits[0], (ROWS, NEW, D), 1.0, 6.0),
        "ln_gain": jnp.clip(1.0 + 0.18 * jax.random.normal(streams_of[1], (LAYERS, D), jnp.float32), 0.1, 1.9),
        "query_weight": scatter_about(streams_of[2], (LAYERS, D, HEADS * HEAD_DIM), D ** -0.5, 0.078125, ((0, 4), (2, 8))),
        "out_weight": scatter_about(streams_of[3], (LAYERS, HEADS * HEAD_DIM, D), (ACTIVE * HEAD_DIM) ** -0.5, 0.15625, ((0, 4), (1, 8))),
        "kv_cache": draw_kv_cache(jax.random.fold_in(jax.random.fold_in(streams_of[7], part), 71), part),
        "new_kv": scatter_about(part_splits[5], (LAYERS, 2, ROWS, NEW, HEADS * HEAD_DIM), 1.0, 6.0, ((0, 4), (4, 8))),
        "active_heads": draw_active_heads(jax.random.fold_in(jax.random.fold_in(streams_of[7], part), 71), part),
    }


epsilon = 1e-05

def layer_norm(values, gain_row):
    floats = values.astype(jnp.float32)
    centre = lax.optimization_barrier(jnp.mean(floats, axis=-1, keepdims=True))
    spread = lax.optimization_barrier(jnp.mean(jnp.square(floats - centre), axis=-1, keepdims=True))
    return ((floats - centre) * lax.rsqrt(spread + epsilon) * gain_row).astype(jnp.bfloat16)

def attend(normed, query_w, cache_keys, cache_values, own_keys, own_values, head_mask, head_dim):
    batch_rows = normed.shape[0]
    positions = normed.shape[1]
    head_count = query_w.shape[1] // head_dim
    queries = jnp.einsum('npd,de->npe', normed.astype(jnp.float32), query_w.astype(jnp.float32))
    queries = (queries * head_dim ** (-0.5)).astype(jnp.bfloat16)
    queries = queries.reshape(batch_rows, positions, head_count, head_dim).astype(jnp.float32)
    keys_past = cache_keys.reshape(batch_rows, cache_keys.shape[1], head_count, head_dim).astype(jnp.float32)
    values_past = cache_values.reshape(batch_rows, cache_values.shape[1], head_count, head_dim).astype(jnp.float32)
    keys_own = own_keys.reshape(batch_rows, positions, head_count, head_dim).astype(jnp.float32)
    values_own = own_values.reshape(batch_rows, positions, head_count, head_dim).astype(jnp.float32)
    cached_scores = jnp.einsum('nphe,nche->nphc', queries, keys_past)
    own_scores = jnp.einsum('nphe,nqhe->nphq', queries, keys_own)
    causal = jnp.arange(positions)[:, None] >= jnp.arange(positions)[None, :]
    own_scores = jnp.where(causal[None, :, None, :], own_scores, jnp.float32(-1e+30))
    top = jnp.maximum(lax.optimization_barrier(jnp.max(cached_scores, axis=-1, keepdims=True)), lax.optimization_barrier(jnp.max(own_scores, axis=-1, keepdims=True)))
    cached_exp = jnp.exp(cached_scores - top)
    own_exp = jnp.exp(own_scores - top)
    total = lax.optimization_barrier(jnp.sum(cached_exp, axis=-1, keepdims=True)) + lax.optimization_barrier(jnp.sum(own_exp, axis=-1, keepdims=True))
    cached_weights = (cached_exp / total).astype(jnp.bfloat16).astype(jnp.float32)
    own_weights = (own_exp / total).astype(jnp.bfloat16).astype(jnp.float32)
    mixed = jnp.einsum('nphc,nche->nphe', cached_weights, values_past)
    mixed = mixed + jnp.einsum('nphq,nqhe->nphe', own_weights, values_own)
    mixed = (mixed * head_mask[:, None, :, None]).astype(jnp.bfloat16)
    return mixed.reshape(batch_rows, positions, head_count * head_dim)

def reference(inputs, ln_gain, query_weight, out_weight, kv_cache, new_kv, active_heads):
    head_on = jnp.any(active_heads[..., None] == jnp.arange(HEADS)[None, None, None, :], axis=2).astype(jnp.float32)
    row_mask = jnp.repeat(head_on, MB_ROWS, axis=0)
    current = inputs
    collected = []
    for layer_index in range(LAYERS):
        normed = layer_norm(current, ln_gain[layer_index])
        attended = attend(normed, query_weight[layer_index], kv_cache[layer_index, 0], kv_cache[layer_index, 1], new_kv[layer_index, 0], new_kv[layer_index, 1], row_mask[:, layer_index], HEAD_DIM)
        partial_sum = jnp.einsum('npe,ed->npd', attended.astype(jnp.float32), out_weight[layer_index].astype(jnp.float32))
        current = (current.astype(jnp.float32) + partial_sum).astype(jnp.bfloat16)
        collected.append(current)
    return jnp.stack(collected)
```

```python
import functools

import jax
import jax.numpy as jnp
from jax import lax
from jax.experimental import pallas as pl
from jax.experimental.pallas import tpu as pltpu
from jax.sharding import PartitionSpec as P

HEAD_DIM = 128
MICRO = 4
MB_ROWS = 8
BATCHES = 1
NEGATIVE = -1e30
EPSILON = 1e-05


def attend_kernel(
    chips, heads, positions, place, active, inputs, *refs
):
    blocks = refs[: 2 * chips]
    gain, query_w, cache, fresh, out = refs[2 * chips :]
    section, chip, core, batch = place[0], place[1], place[2], place[3]
    width = blocks[0].shape[1]
    model = width * 2 * chips
    tokens = inputs.shape[0]
    first = section == 0
    places = []
    for index in range(2 * chips):
        source = lax.rem(chip + chips - index % chips, chips)
        parity = core if index < chips else 1 - core
        places.append(pl.multiple_of((2 * source + parity) * width, 128))

    def block(index):
        given = inputs[:, pl.ds(places[index], width)]
        return jnp.where(first, given, blocks[index][...]).astype(jnp.float32)

    total = jnp.zeros((tokens, 1), jnp.float32)
    for index in range(2 * chips):
        total += jnp.sum(block(index), axis=1, keepdims=True)
    centre = total / model
    total = jnp.zeros((tokens, 1), jnp.float32)
    for index in range(2 * chips):
        total += jnp.sum(jnp.square(block(index) - centre), axis=1, keepdims=True)
    scale = lax.rsqrt(total / model + EPSILON)
    queries = jnp.zeros((tokens, heads * HEAD_DIM), jnp.float32)
    for index in range(2 * chips):
        normed = (block(index) - centre) * scale * gain[:, pl.ds(places[index], width)]
        queries += jnp.dot(
            normed.astype(jnp.bfloat16),
            query_w[pl.ds(places[index], width), :],
            preferred_element_type=jnp.float32,
        )
    queries = (queries * HEAD_DIM ** (-0.5)).astype(jnp.bfloat16)

    group = MB_ROWS * positions
    groups = tokens // group
    past = cache.shape[2]
    row_at = lax.broadcasted_iota(jnp.int32, (group, MB_ROWS * past), 0)
    column_at = lax.broadcasted_iota(jnp.int32, (group, MB_ROWS * past), 1)
    cached_mask = row_at // positions == column_at // past
    row_at = lax.broadcasted_iota(jnp.int32, (group, group), 0)
    column_at = lax.broadcasted_iota(jnp.int32, (group, group), 1)
    own_mask = (row_at // positions == column_at // positions) & (column_at <= row_at)
    transposed = (((1,), (1,)), ((), ()))
    for micro in range(groups):
        micro_at = batch * groups + micro
        rows = pl.ds(micro_at * MB_ROWS, MB_ROWS)
        fresh_rows = pl.ds(pl.multiple_of(micro_at * group, group), group)
        for head in range(heads):
            lanes = slice(head * HEAD_DIM, (head + 1) * HEAD_DIM)
            name = (2 * chip + core) * heads + head
            active_now = active[micro_at, section, 0] == name
            for entry in range(1, active.shape[2]):
                active_now |= active[micro_at, section, entry] == name
            query = queries[micro * group : (micro + 1) * group, lanes]
            keys = cache[0, rows, :, lanes].reshape(MB_ROWS * past, HEAD_DIM)
            values = cache[1, rows, :, lanes].reshape(MB_ROWS * past, HEAD_DIM)
            own_keys = fresh[0, fresh_rows, lanes]
            own_values = fresh[1, fresh_rows, lanes]
            cached = lax.dot_general(query, keys, transposed, preferred_element_type=jnp.float32)
            own = lax.dot_general(query, own_keys, transposed, preferred_element_type=jnp.float32)
            cached = jnp.where(cached_mask, cached, NEGATIVE)
            own = jnp.where(own_mask, own, NEGATIVE)
            top = jnp.maximum(
                jnp.max(cached, axis=1, keepdims=True), jnp.max(own, axis=1, keepdims=True)
            )
            cached = jnp.exp(cached - top)
            own = jnp.exp(own - top)
            weight = 1.0 / (
                jnp.sum(cached, axis=1, keepdims=True) + jnp.sum(own, axis=1, keepdims=True)
            )
            mixed = jnp.dot(
                (cached * weight).astype(jnp.bfloat16), values, preferred_element_type=jnp.float32
            )
            mixed += jnp.dot(
                (own * weight).astype(jnp.bfloat16), own_values, preferred_element_type=jnp.float32
            )
            mixed = jnp.where(active_now, mixed, 0.0)
            out[micro * group : (micro + 1) * group, lanes] = mixed.astype(jnp.bfloat16)


def project_kernel(chips, place, own, other, own_w, other_w, *outs):
    chip, core = place[1], place[2]
    width = outs[0].shape[1]
    for index in range(chips):
        target = lax.rem(chip + index, chips)
        columns = pl.ds(pl.multiple_of((2 * target + core) * width, 128), width)
        result = jnp.dot(own[...], own_w[:, columns], preferred_element_type=jnp.float32)
        result += jnp.dot(other[...], other_w[:, columns], preferred_element_type=jnp.float32)
        outs[index][...] = result.astype(outs[index].dtype)


VMEM = pl.BlockSpec(memory_space=pltpu.VMEM)
SMEM = pl.BlockSpec(memory_space=pltpu.SMEM)
LIMIT = pltpu.CompilerParams(vmem_limit_bytes=40 * 2**20)


def on_device(inputs, ln_gain, query_weight, out_weight, kv_cache, new_kv, active_heads):
    tensor_size = lax.axis_size("tensor")
    pipe_size = lax.axis_size("pipe")
    chips = tensor_size // 2
    section = lax.axis_index("pipe")
    slot = lax.axis_index("tensor")
    chip, core = slot // 2, slot % 2
    rows, positions, model = inputs.shape
    width = model // tensor_size
    heads = query_weight.shape[2] // HEAD_DIM
    tokens = rows * positions // BATCHES
    query_w = query_weight[0]
    own_w = out_weight[0]
    swap = [(i, i ^ 1) for i in range(tensor_size)]
    other_w = lax.ppermute(own_w, "tensor", swap)
    cache = kv_cache[0]
    fresh = new_kv[0].reshape(2, rows * positions, heads * HEAD_DIM)
    flat = inputs.reshape(rows * positions, model)

    def along(value, by):
        pairs = [(i, (i + 2 * by) % tensor_size) for i in range(tensor_size)]
        return lax.ppermute(value, "tensor", pairs)

    def onward(value, by):
        pairs = [
            (p * tensor_size + i, (p + 1) * tensor_size + (i + 2 * by) % tensor_size)
            for p in range(pipe_size - 1)
            for i in range(tensor_size)
        ]
        return lax.ppermute(value, ("pipe", "tensor"), pairs)

    attend = pl.pallas_call(
        functools.partial(attend_kernel, chips, heads, positions),
        out_shape=jax.ShapeDtypeStruct((tokens, heads * HEAD_DIM), jnp.bfloat16),
        in_specs=[SMEM] * 2 + [VMEM] * (2 * chips + 5),
        out_specs=VMEM,
        compiler_params=LIMIT,
    )
    project = pl.pallas_call(
        functools.partial(project_kernel, chips),
        out_shape=[
            jax.ShapeDtypeStruct((tokens, width), jnp.float32 if k == 0 else jnp.bfloat16)
            for k in range(chips)
        ],
        in_specs=[SMEM] + [VMEM] * 4,
        out_specs=[VMEM] * chips,
        compiler_params=LIMIT,
    )
    blank = jnp.zeros((tokens, width), jnp.bfloat16)
    blocks = [blank] * tensor_size
    results = [blank] * BATCHES
    steps = BATCHES + pipe_size - 1
    for step in range(steps):
        batch = jnp.clip(step - section, 0, BATCHES - 1)
        place = jnp.stack([section, chip, core, batch]).astype(jnp.int32)
        start = min(step, BATCHES - 1) * tokens
        given = flat[start : start + tokens]
        attended = attend(place, active_heads, given, *blocks, ln_gain, query_w, cache, fresh)
        other = lax.ppermute(attended, "tensor", swap)
        parts = project(place, attended, other, own_w, other_w)
        summed = parts[0]
        for index in range(1, chips):
            summed = summed + along(parts[index], index).astype(jnp.float32)
        own_given = lax.dynamic_slice_in_dim(given, slot * width, width, 1)
        current = jnp.where(section == 0, own_given, blocks[0])
        updated = (current.astype(jnp.float32) + summed).astype(jnp.bfloat16)
        for index in range(BATCHES):
            results[index] = jnp.where(section + index == step, updated, results[index])
        if step + 1 < steps:
            blocks = [onward(updated, index) for index in range(chips)]
            blocks += [lax.ppermute(block, "tensor", swap) for block in blocks]
    result = jnp.concatenate(results, axis=0)
    return result.reshape(1, rows, positions, width)


def solution(mesh):
    return jax.shard_map(
        on_device,
        mesh=mesh,
        in_specs=(
            P("dp", None, None),
            P("pipe", None),
            P("pipe", None, "tensor"),
            P("pipe", "tensor", None),
            P("pipe", None, "dp", None, "tensor"),
            P("pipe", None, "dp", None, "tensor"),
            P("dp", None, None),
        ),
        out_specs=P("pipe", "dp", None, "tensor"),
        check_vma=False,
    )
```

```python
import functools

import jax
import jax.numpy as jnp
from jax import lax
from jax.experimental import pallas as pl
from jax.experimental.pallas import tpu as pltpu
from jax.sharding import PartitionSpec as P

HEAD_DIM = 128
MB_ROWS = 8
NEGATIVE = -1e30
EPSILON = 1e-05
SCALE = HEAD_DIM ** (-0.5)
ORDER = (2, 1, 3, 0)
ARRIVALS = (0, 1, 3, 2)
GROUP_ROWS = 4


def normed_queries(blocks, gains, weights):
    tokens = blocks[0].shape[0]
    model = sum(block.shape[1] for block in blocks)
    total = jnp.zeros((tokens, 1), jnp.float32)
    for block in blocks:
        total += jnp.sum(block, axis=1, keepdims=True)
    centre = total / model
    total = jnp.zeros((tokens, 1), jnp.float32)
    for block in blocks:
        total += jnp.sum(jnp.square(block - centre), axis=1, keepdims=True)
    scale = lax.rsqrt(total / model + EPSILON)
    queries = 0.0
    for block, gain, weight in zip(blocks, gains, weights):
        normed = ((block - centre) * scale * gain).astype(jnp.bfloat16)
        queries += jnp.dot(normed, weight(), preferred_element_type=jnp.float32)
    return (queries * SCALE).astype(jnp.bfloat16)


def attention(place, active, queries, cache, fresh, positions):
    section, name_base = place[0], place[3]
    tokens = queries.shape[0]
    heads = queries.shape[1] // HEAD_DIM
    past = cache.shape[2]
    group = GROUP_ROWS * positions
    row_at = lax.broadcasted_iota(jnp.int32, (group, GROUP_ROWS * past), 0)
    column_at = lax.broadcasted_iota(jnp.int32, (group, GROUP_ROWS * past), 1)
    cached_mask = row_at // positions == column_at // past
    row_at = lax.broadcasted_iota(jnp.int32, (tokens, tokens), 0)
    column_at = lax.broadcasted_iota(jnp.int32, (tokens, tokens), 1)
    own_mask = (row_at // positions == column_at // positions) & (column_at <= row_at)
    transposed = (((1,), (1,)), ((), ()))
    groups = [
        (slice(at * GROUP_ROWS, (at + 1) * GROUP_ROWS), slice(at * group, (at + 1) * group))
        for at in range(tokens // group)
    ]
    lanes = [slice(head * HEAD_DIM, (head + 1) * HEAD_DIM) for head in range(heads)]
    scores = []
    for lane in lanes:
        own = lax.dot_general(
            queries[:, lane], fresh[0, :, lane], transposed, preferred_element_type=jnp.float32
        )
        cached = []
        for rows, here in groups:
            keys = cache[0, rows, :, lane].reshape(GROUP_ROWS * past, HEAD_DIM)
            score = lax.dot_general(
                queries[here, lane], keys, transposed, preferred_element_type=jnp.float32
            )
            cached.append(jnp.where(cached_mask, score, NEGATIVE))
        scores.append((jnp.where(own_mask, own, NEGATIVE), cached))
    weights = []
    for own, cached in scores:
        own_weights, cached_weights = [], []
        for score, (_, here) in zip(cached, groups):
            new = own[here]
            top = jnp.maximum(
                jnp.max(score, axis=1, keepdims=True), jnp.max(new, axis=1, keepdims=True)
            )
            score = jnp.exp(score - top)
            new = jnp.exp(new - top)
            share = 1.0 / (
                jnp.sum(score, axis=1, keepdims=True) + jnp.sum(new, axis=1, keepdims=True)
            )
            cached_weights.append((score * share).astype(jnp.bfloat16))
            own_weights.append((new * share).astype(jnp.bfloat16))
        weights.append((jnp.concatenate(own_weights, axis=0), cached_weights))
    result = []
    for head, (lane, (own, cached)) in enumerate(zip(lanes, weights)):
        mixed = jnp.dot(own, fresh[1, :, lane], preferred_element_type=jnp.float32)
        parts = []
        for weight, (rows, here) in zip(cached, groups):
            values = cache[1, rows, :, lane].reshape(GROUP_ROWS * past, HEAD_DIM)
            part = mixed[here] + jnp.dot(weight, values, preferred_element_type=jnp.float32)
            micro = rows.start // MB_ROWS
            active_now = active[micro, section, 0] == name_base + head
            for entry in range(1, active.shape[2]):
                active_now |= active[micro, section, entry] == name_base + head
            parts.append(jnp.where(active_now, part, 0.0).astype(jnp.bfloat16))
        result.append(jnp.concatenate(parts, axis=0))
    return result


def opening_kernel(
    place, active_in, inputs, gain_in, query_w, cache, new, own_w,
    kept, given_first, given_second, own_block, query_out, cache_out, fresh_out, keep_w, give_w,
    active, held, gain, new_held, sems,
):
    rows, positions, model = held.shape
    tokens = rows * positions
    chip, core, chips = place[1], place[2], place[4]
    width = own_block.shape[1]
    parts = 4
    depth = model // parts
    loads = [pltpu.make_async_copy(inputs, held, sems.at[0])]
    small = [
        pltpu.make_async_copy(gain_in, gain, sems.at[parts + 3]),
        pltpu.make_async_copy(active_in, active, sems.at[parts + 4]),
    ]
    for part in range(parts):
        span = pl.ds(part * depth, depth)
        loads.append(
            pltpu.make_async_copy(query_w.at[0, span, :], query_out.at[span, :], sems.at[1 + part])
        )
    loads.append(pltpu.make_async_copy(new.at[0], new_held, sems.at[parts + 1]))
    loads.append(pltpu.make_async_copy(cache.at[0], cache_out, sems.at[parts + 2]))
    for at, index in enumerate(ORDER):
        target = lax.rem(chip + index, chips)
        to = pl.ds(at * width, width)
        for side, held_w in ((core, keep_w), (1 - core, give_w)):
            columns = pl.ds(pl.multiple_of((2 * target + side) * width, 128), width)
            load = pltpu.make_async_copy(
                own_w.at[0, :, columns], held_w.at[:, to], sems.at[parts + 5 + len(loads)]
            )
            loads.append(load)
    for load in small + loads:
        load.start()
    loads[0].wait()
    small[0].wait()
    blocks, gains, weights = [], [], []
    for part in range(parts):
        span = slice(part * depth, (part + 1) * depth)
        blocks.append(held[:, :, span].reshape(tokens, depth).astype(jnp.float32))
        gains.append(gain[:, span])

        def weight(part=part, span=span):
            loads[1 + part].wait()
            return query_out[span, :]

        weights.append(weight)
    start = pl.multiple_of((2 * chip + core) * width, 128)
    own_block[...] = held[:, :, pl.ds(start, width)].reshape(tokens, width)
    queries = normed_queries(blocks, gains, weights)
    loads[parts + 1].wait()
    fresh_out[0] = new_held[0].reshape(tokens, fresh_out.shape[2])
    fresh_out[1] = new_held[1].reshape(tokens, fresh_out.shape[2])
    loads[parts + 2].wait()
    small[1].wait()
    attended = jnp.concatenate(
        attention(place, active, queries, cache_out, fresh_out, positions), axis=1
    )
    for load in loads[parts + 3 :]:
        load.wait()
    given = jnp.dot(attended, give_w[...], preferred_element_type=jnp.float32)
    given_first[...] = given[:, : 2 * width].astype(given_first.dtype)
    given_second[...] = given[:, 2 * width :].astype(given_second.dtype)
    kept[...] = jnp.dot(attended, keep_w[...], preferred_element_type=jnp.float32)


def give(parts, outs, current):
    if current is not None:
        parts[1] += current[...].astype(jnp.float32)
    for part, out in zip(parts, outs):
        out[...] = part.astype(out.dtype)


def merge_kernel(kept, taken, *refs):
    current, outs = (None, refs) if len(refs) == 2 else (refs[0], refs[1:])
    width = outs[0].shape[1]
    first = 0 if current is None else 2
    parts = []
    for at in range(2):
        here = slice(at * width, (at + 1) * width)
        there = slice((first + at) * width, (first + at + 1) * width)
        parts.append(kept[:, there] + taken[:, here].astype(jnp.float32))
    give(parts, outs, current)


def layer_kernel(positions, place, active, *refs):
    blocks = refs[:-5]
    gain, query_w, cache, fresh, out = refs[-5:]
    chip, core, chips = place[1], place[2], place[4]
    width = blocks[0].shape[1]
    values, gains, weights = [], [], []
    for at, block in enumerate(blocks):
        source = lax.rem(chip + chips - ARRIVALS[at // 2], chips)
        side = core if at % 2 == 0 else 1 - core
        span = pl.ds(pl.multiple_of((2 * source + side) * width, 128), width)
        values.append(block[...].astype(jnp.float32))
        gains.append(gain[:, span])
        weights.append(lambda span=span: query_w[span, :])
    queries = normed_queries(values, gains, weights)
    for head, mixed in enumerate(attention(place, active, queries, cache, fresh, positions)):
        out[:, head * HEAD_DIM : (head + 1) * HEAD_DIM] = mixed


def project_kernel(own, other, keep_w, take_w, *refs):
    current, outs = (None, refs) if len(refs) == 2 else (refs[0], refs[1:])
    width = outs[0].shape[1]
    first = 0 if current is None else 2
    columns = slice(first * width, (first + 2) * width)
    result = jnp.dot(own[...], keep_w[:, columns], preferred_element_type=jnp.float32)
    result += jnp.dot(other[...], take_w[:, columns], preferred_element_type=jnp.float32)
    give([result[:, :width], result[:, width:]], outs, current)


VMEM = pl.BlockSpec(memory_space=pltpu.VMEM)
SMEM = pl.BlockSpec(memory_space=pltpu.SMEM)
HBM = pl.BlockSpec(memory_space=pltpu.HBM)


def call(kernel, scalars, *args, outs, space=VMEM, scratch=(), flops=0):
    moved = sum(a.size * a.dtype.itemsize for a in args)
    if space is HBM:
        args = [pltpu.with_memory_space_constraint(a, pltpu.HBM) for a in args]
    return pl.pallas_call(
        kernel,
        out_shape=[jax.ShapeDtypeStruct(shape, kind) for shape, kind in outs],
        in_specs=[SMEM] * len(scalars) + [space] * len(args),
        out_specs=[VMEM] * len(outs),
        scratch_shapes=scratch,
        compiler_params=pltpu.CompilerParams(vmem_limit_bytes=24 * 2**20),
        cost_estimate=pl.CostEstimate(flops=flops, bytes_accessed=moved, transcendentals=0),
    )(*scalars, *args)


def on_device(inputs, ln_gain, query_weight, out_weight, kv_cache, new_kv, active_heads):
    tensor_size = lax.axis_size("tensor")
    pipe_size = lax.axis_size("pipe")
    chips = tensor_size // 2
    section = lax.axis_index("pipe")
    slot = lax.axis_index("tensor")
    rows, positions, model = inputs.shape
    width = model // tensor_size
    tokens = rows * positions
    inner = query_weight.shape[2]
    heads = inner // HEAD_DIM
    past = kv_cache.shape[3]
    swap = [(i, i ^ 1) for i in range(tensor_size)]
    place = jnp.stack([section, slot // 2, slot % 2, slot * heads, chips]).astype(jnp.int32)

    def across(value):
        return lax.ppermute(value, "tensor", swap)

    def send(value, by, stages):
        pairs = []
        for stage in range(pipe_size):
            for at in range(tensor_size):
                target = (stage + stages) % pipe_size * tensor_size + (at + 2 * by) % tensor_size
                pairs.append((stage * tensor_size + at, target))
        return lax.ppermute(value, ("pipe", "tensor"), pairs)

    half, full = jnp.bfloat16, jnp.float32
    chunk = ((tokens, width), half)
    kept_chunk = ((tokens, width), full)
    last_outs = [chunk, kept_chunk]
    kept, given_first, given_second, current, query_w, cache, fresh, keep_w, give_w = call(
        opening_kernel,
        (place,),
        active_heads,
        inputs,
        ln_gain,
        query_weight,
        kv_cache,
        new_kv,
        out_weight,
        space=HBM,
        outs=[
            ((tokens, chips * width), full),
            ((tokens, 2 * width), half),
            ((tokens, 2 * width), half),
            chunk,
            ((model, inner), half),
            ((2, rows, past, inner), half),
            ((2, tokens, inner), half),
            ((inner, chips * width), half),
            ((inner, chips * width), half),
        ],
        scratch=[
            pltpu.SMEM(active_heads.shape, jnp.int32),
            pltpu.VMEM((rows, positions, model), half),
            pltpu.VMEM((1, model), full),
            pltpu.VMEM((2, rows, positions, inner), half),
            pltpu.SemaphoreType.DMA((17 + 2 * chips,)),
        ],
    )
    sent = call(merge_kernel, (), kept, across(given_first), outs=[chunk, chunk])
    last = call(merge_kernel, (), kept, across(given_second), current, outs=last_outs)
    give_w, _ = lax.optimization_barrier((give_w, last))
    take_w = across(give_w)
    result = None
    for step in range(pipe_size):
        if step > 0:
            arrived = {index: send(updated, index, 1) for index in ARRIVALS}
            current = arrived[0]
            blocks = [b for i in ARRIVALS for b in (arrived[i], across(arrived[i]))]
            [attended] = call(
                functools.partial(layer_kernel, positions),
                (place, active_heads),
                *blocks,
                ln_gain,
                query_w,
                cache,
                fresh,
                outs=[((tokens, inner), half)],
            )
            other = across(attended)
            factors = (attended, other, keep_w, take_w)
            sent = call(project_kernel, (), *factors, outs=[chunk, chunk])
            last = call(project_kernel, (), *factors, current, outs=last_outs)
        summed = last[1]
        for index, part in zip(ORDER, (*sent, last[0])):
            summed = summed + send(part, index, 0).astype(full)
        updated = summed.astype(half)
        result = updated if result is None else jnp.where(section == step, updated, result)
    return result.reshape(1, rows, positions, width)


def solution(mesh):
    return jax.shard_map(
        on_device,
        mesh=mesh,
        in_specs=(
            P("dp", None, None),
            P("pipe", None),
            P("pipe", None, "tensor"),
            P("pipe", "tensor", None),
            P("pipe", None, "dp", None, "tensor"),
            P("pipe", None, "dp", None, "tensor"),
            P("dp", None, None),
        ),
        out_specs=P("pipe", "dp", None, "tensor"),
        check_vma=False,
    )
```

```python
import functools

import jax
import jax.numpy as jnp
from jax import lax
from jax.experimental import pallas as pl
from jax.experimental.pallas import tpu as pltpu
from jax.sharding import PartitionSpec as P

HEAD_DIM = 128
MB_ROWS = 8
NEGATIVE = -1e30
EPSILON = 1e-05
SCALE = HEAD_DIM ** (-0.5)
ORDER = (2, 1, 3, 0)
ARRIVALS = (0, 2, 1, 3)
GROUP_ROWS = 4


def normed_queries(blocks, gains, weights):
    tokens = blocks[0].shape[0]
    model = sum(block.shape[1] for block in blocks)
    total = jnp.zeros((tokens, 1), jnp.float32)
    for block in blocks:
        total += jnp.sum(block, axis=1, keepdims=True)
    centre = total / model
    total = jnp.zeros((tokens, 1), jnp.float32)
    for block in blocks:
        total += jnp.sum(jnp.square(block - centre), axis=1, keepdims=True)
    scale = lax.rsqrt(total / model + EPSILON)
    queries = 0.0
    for block, gain, weight in zip(blocks, gains, weights):
        normed = ((block - centre) * scale * gain).astype(jnp.bfloat16)
        queries += jnp.dot(normed, weight(), preferred_element_type=jnp.float32)
    return (queries * SCALE).astype(jnp.bfloat16)


def attention(place, active, queries, cache, fresh, positions):
    section, name_base = place[0], place[3]
    tokens = queries.shape[0]
    heads = queries.shape[1] // HEAD_DIM
    past = cache.shape[2]
    group = GROUP_ROWS * positions
    row_at = lax.broadcasted_iota(jnp.int32, (group, GROUP_ROWS * past), 0)
    column_at = lax.broadcasted_iota(jnp.int32, (group, GROUP_ROWS * past), 1)
    cached_mask = row_at // positions == column_at // past
    row_at = lax.broadcasted_iota(jnp.int32, (tokens, tokens), 0)
    column_at = lax.broadcasted_iota(jnp.int32, (tokens, tokens), 1)
    own_mask = (row_at // positions == column_at // positions) & (column_at <= row_at)
    transposed = (((1,), (1,)), ((), ()))
    groups = [
        (slice(at * GROUP_ROWS, (at + 1) * GROUP_ROWS), slice(at * group, (at + 1) * group))
        for at in range(tokens // group)
    ]
    lanes = [slice(head * HEAD_DIM, (head + 1) * HEAD_DIM) for head in range(heads)]
    scores = []
    for lane in lanes:
        own = lax.dot_general(
            queries[:, lane], fresh[0, :, lane], transposed, preferred_element_type=jnp.float32
        )
        cached = []
        for rows, here in groups:
            keys = cache[0, rows, :, lane].reshape(GROUP_ROWS * past, HEAD_DIM)
            score = lax.dot_general(
                queries[here, lane], keys, transposed, preferred_element_type=jnp.float32
            )
            cached.append(jnp.where(cached_mask, score, NEGATIVE))
        scores.append((jnp.where(own_mask, own, NEGATIVE), cached))
    weights = []
    for own, cached in scores:
        own_weights, cached_weights = [], []
        for score, (_, here) in zip(cached, groups):
            new = own[here]
            top = jnp.maximum(
                jnp.max(score, axis=1, keepdims=True), jnp.max(new, axis=1, keepdims=True)
            )
            score = jnp.exp(score - top)
            new = jnp.exp(new - top)
            share = 1.0 / (
                jnp.sum(score, axis=1, keepdims=True) + jnp.sum(new, axis=1, keepdims=True)
            )
            cached_weights.append((score * share).astype(jnp.bfloat16))
            own_weights.append((new * share).astype(jnp.bfloat16))
        weights.append((jnp.concatenate(own_weights, axis=0), cached_weights))
    result = []
    for head, (lane, (own, cached)) in enumerate(zip(lanes, weights)):
        mixed = jnp.dot(own, fresh[1, :, lane], preferred_element_type=jnp.float32)
        parts = []
        for weight, (rows, here) in zip(cached, groups):
            values = cache[1, rows, :, lane].reshape(GROUP_ROWS * past, HEAD_DIM)
            part = mixed[here] + jnp.dot(weight, values, preferred_element_type=jnp.float32)
            micro = rows.start // MB_ROWS
            active_now = active[micro, section, 0] == name_base + head
            for entry in range(1, active.shape[2]):
                active_now |= active[micro, section, entry] == name_base + head
            parts.append(jnp.where(active_now, part, 0.0).astype(jnp.bfloat16))
        result.append(jnp.concatenate(parts, axis=0))
    return result


def opening_kernel(
    place, active_in, inputs, gain_in, query_w, cache, new, own_w,
    kept, given_out, own_block, query_out, cache_out, fresh_out, keep_w, give_w,
    active, held, gain, new_held, sems,
):
    rows, positions, model = held.shape
    tokens = rows * positions
    chip, core, chips = place[1], place[2], place[4]
    width = own_block.shape[1]
    parts = 4
    depth = model // parts
    loads = [pltpu.make_async_copy(inputs, held, sems.at[0])]
    small = [
        pltpu.make_async_copy(gain_in, gain, sems.at[parts + 3]),
        pltpu.make_async_copy(active_in, active, sems.at[parts + 4]),
    ]
    for part in range(parts):
        span = pl.ds(part * depth, depth)
        loads.append(
            pltpu.make_async_copy(query_w.at[0, span, :], query_out.at[span, :], sems.at[1 + part])
        )
    loads.append(pltpu.make_async_copy(new.at[0], new_held, sems.at[parts + 1]))
    loads.append(pltpu.make_async_copy(cache.at[0], cache_out, sems.at[parts + 2]))
    for at, index in enumerate(ORDER):
        target = lax.rem(chip + index, chips)
        to = pl.ds(at * width, width)
        for side, held_w in ((core, keep_w), (1 - core, give_w)):
            columns = pl.ds(pl.multiple_of((2 * target + side) * width, 128), width)
            load = pltpu.make_async_copy(
                own_w.at[0, :, columns], held_w.at[:, to], sems.at[parts + 5 + len(loads)]
            )
            loads.append(load)
    for load in small + loads:
        load.start()
    loads[0].wait()
    small[0].wait()
    blocks, gains, weights = [], [], []
    for part in range(parts):
        span = slice(part * depth, (part + 1) * depth)
        blocks.append(held[:, :, span].reshape(tokens, depth).astype(jnp.float32))
        gains.append(gain[:, span])

        def weight(part=part, span=span):
            loads[1 + part].wait()
            return query_out[span, :]

        weights.append(weight)
    start = pl.multiple_of((2 * chip + core) * width, 128)
    own_block[...] = held[:, :, pl.ds(start, width)].reshape(tokens, width)
    queries = normed_queries(blocks, gains, weights)
    loads[parts + 1].wait()
    fresh_out[0] = new_held[0].reshape(tokens, fresh_out.shape[2])
    fresh_out[1] = new_held[1].reshape(tokens, fresh_out.shape[2])
    loads[parts + 2].wait()
    small[1].wait()
    attended = jnp.concatenate(
        attention(place, active, queries, cache_out, fresh_out, positions), axis=1
    )
    for load in loads[parts + 3 :]:
        load.wait()
    given = jnp.dot(attended, give_w[...], preferred_element_type=jnp.float32)
    given_out[...] = given.astype(given_out.dtype)
    kept[...] = jnp.dot(attended, keep_w[...], preferred_element_type=jnp.float32)


def give(parts, outs, current):
    if current is not None:
        parts[1] += current[...].astype(jnp.float32)
    for part, out in zip(parts, outs):
        out[...] = part.astype(out.dtype)


def merge_kernel(kept, taken, current, weights, *outs):
    del weights
    width = current.shape[1]
    for at, out in enumerate(outs[:-1]):
        here = slice(at * width, (at + 1) * width)
        part = kept[:, here] + taken[:, here].astype(jnp.float32)
        if at == len(ORDER) - 1:
            part += current[...].astype(jnp.float32)
        out[...] = part.astype(out.dtype)


def layer_kernel(positions, place, active, *refs):
    blocks = refs[:-5]
    gain, query_w, cache, fresh, out = refs[-5:]
    chip, core, chips = place[1], place[2], place[4]
    width = blocks[0].shape[1]
    values, gains, weights = [], [], []
    for at, block in enumerate(blocks):
        source = lax.rem(chip + chips - ARRIVALS[at // 2], chips)
        side = core if at % 2 == 0 else 1 - core
        span = pl.ds(pl.multiple_of((2 * source + side) * width, 128), width)
        values.append(block[...].astype(jnp.float32))
        gains.append(gain[:, span])
        weights.append(lambda span=span: query_w[span, :])
    queries = normed_queries(values, gains, weights)
    for head, mixed in enumerate(attention(place, active, queries, cache, fresh, positions)):
        out[:, head * HEAD_DIM : (head + 1) * HEAD_DIM] = mixed


def project_kernel(own, other, keep_w, take_w, *refs):
    current, outs = (None, refs) if len(refs) == 2 else (refs[0], refs[1:])
    width = outs[0].shape[1]
    first = 0 if current is None else 2
    columns = slice(first * width, (first + 2) * width)
    result = jnp.dot(own[...], keep_w[:, columns], preferred_element_type=jnp.float32)
    result += jnp.dot(other[...], take_w[:, columns], preferred_element_type=jnp.float32)
    give([result[:, :width], result[:, width:]], outs, current)


VMEM = pl.BlockSpec(memory_space=pltpu.VMEM)
SMEM = pl.BlockSpec(memory_space=pltpu.SMEM)
HBM = pl.BlockSpec(memory_space=pltpu.HBM)


def call(kernel, scalars, *args, outs, space=VMEM, scratch=(), flops=0, passed=False):
    spaces = [space] * len(args)
    out_spaces = [VMEM] * len(outs)
    aliases = {}
    if passed:
        spaces[-1] = out_spaces[-1] = pl.BlockSpec(memory_space=pl.ANY)
        aliases = {len(scalars) + len(args) - 1: len(outs) - 1}
    moved = sum(a.size * a.dtype.itemsize for a in args)
    if space is HBM:
        args = [pltpu.with_memory_space_constraint(a, pltpu.HBM) for a in args]
    return pl.pallas_call(
        kernel,
        out_shape=[jax.ShapeDtypeStruct(shape, kind) for shape, kind in outs],
        in_specs=[SMEM] * len(scalars) + spaces,
        out_specs=out_spaces,
        input_output_aliases=aliases,
        scratch_shapes=scratch,
        compiler_params=pltpu.CompilerParams(vmem_limit_bytes=24 * 2**20),
        cost_estimate=pl.CostEstimate(flops=flops, bytes_accessed=moved, transcendentals=0),
    )(*scalars, *args)


def on_device(inputs, ln_gain, query_weight, out_weight, kv_cache, new_kv, active_heads):
    tensor_size = lax.axis_size("tensor")
    pipe_size = lax.axis_size("pipe")
    chips = tensor_size // 2
    section = lax.axis_index("pipe")
    slot = lax.axis_index("tensor")
    rows, positions, model = inputs.shape
    width = model // tensor_size
    tokens = rows * positions
    inner = query_weight.shape[2]
    heads = inner // HEAD_DIM
    past = kv_cache.shape[3]
    swap = [(i, i ^ 1) for i in range(tensor_size)]
    place = jnp.stack([section, slot // 2, slot % 2, slot * heads, chips]).astype(jnp.int32)

    def across(value):
        return lax.ppermute(value, "tensor", swap)

    def send(value, by, stages):
        pairs = []
        for stage in range(pipe_size):
            for at in range(tensor_size):
                target = (stage + stages) % pipe_size * tensor_size + (at + 2 * by) % tensor_size
                pairs.append((stage * tensor_size + at, target))
        return lax.ppermute(value, ("pipe", "tensor"), pairs)

    half, full = jnp.bfloat16, jnp.float32
    chunk = ((tokens, width), half)
    kept_chunk = ((tokens, width), full)
    last_outs = [chunk, kept_chunk]
    kept, given, current, query_w, cache, fresh, keep_w, give_w = call(
        opening_kernel,
        (place,),
        active_heads,
        inputs,
        ln_gain,
        query_weight,
        kv_cache,
        new_kv,
        out_weight,
        space=HBM,
        outs=[
            ((tokens, chips * width), full),
            ((tokens, chips * width), half),
            chunk,
            ((model, inner), half),
            ((2, rows, past, inner), half),
            ((2, tokens, inner), half),
            ((inner, chips * width), half),
            ((inner, chips * width), half),
        ],
        scratch=[
            pltpu.SMEM(active_heads.shape, jnp.int32),
            pltpu.VMEM((rows, positions, model), half),
            pltpu.VMEM((1, model), full),
            pltpu.VMEM((2, rows, positions, inner), half),
            pltpu.SemaphoreType.DMA((17 + 2 * chips,)),
        ],
    )
    *sent, last_chunk, own_chunk, give_w = call(
        merge_kernel,
        (),
        kept,
        across(given),
        current,
        give_w,
        outs=[chunk, chunk, chunk, kept_chunk, ((inner, chips * width), half)],
        passed=True,
    )
    last = [last_chunk, own_chunk]
    take_w = across(give_w)
    result = None
    for step in range(pipe_size):
        if step > 0:
            hopped = send(updated, 0, 1)
            arrived = {0: hopped, **{index: send(hopped, index, 0) for index in ORDER[:3]}}
            current = arrived[0]
            blocks = [b for i in ARRIVALS for b in (arrived[i], across(arrived[i]))]
            [attended] = call(
                functools.partial(layer_kernel, positions),
                (place, active_heads),
                *blocks,
                ln_gain,
                query_w,
                cache,
                fresh,
                outs=[((tokens, inner), half)],
            )
            other = across(attended)
            factors = (attended, other, keep_w, take_w)
            sent = call(project_kernel, (), *factors, outs=[chunk, chunk])
            last = call(project_kernel, (), *factors, current, outs=last_outs)
        summed = last[1]
        for index, part in zip(ORDER, (*sent, last[0])):
            summed = summed + send(part, index, 0).astype(full)
        updated = summed.astype(half)
        result = updated if result is None else jnp.where(section == step, updated, result)
    return result.reshape(1, rows, positions, width)


def solution(mesh):
    return jax.shard_map(
        on_device,
        mesh=mesh,
        in_specs=(
            P("dp", None, None),
            P("pipe", None),
            P("pipe", None, "tensor"),
            P("pipe", "tensor", None),
            P("pipe", None, "dp", None, "tensor"),
            P("pipe", None, "dp", None, "tensor"),
            P("dp", None, None),
        ),
        out_specs=P("pipe", "dp", None, "tensor"),
        check_vma=False,
    )
```

```python
import functools

import jax
import jax.numpy as jnp
from jax import lax
from jax.experimental import pallas as pl
from jax.experimental.pallas import tpu as pltpu
from jax.sharding import PartitionSpec as P

HEAD_DIM = 128
MB_ROWS = 8
NEGATIVE = -1e30
EPSILON = 1e-05
SCALE = HEAD_DIM ** (-0.5)
ORDER = (2, 1, 3, 0)
ARRIVALS = (0, 2, 1, 3)
GROUP_ROWS = 4


def normed_queries(blocks, gains, weights):
    tokens = blocks[0].shape[0]
    model = sum(block.shape[1] for block in blocks)
    total = jnp.zeros((tokens, 1), jnp.float32)
    for block in blocks:
        total += jnp.sum(block, axis=1, keepdims=True)
    centre = total / model
    total = jnp.zeros((tokens, 1), jnp.float32)
    for block in blocks:
        total += jnp.sum(jnp.square(block - centre), axis=1, keepdims=True)
    scale = lax.rsqrt(total / model + EPSILON)
    queries = 0.0
    for block, gain, weight in zip(blocks, gains, weights):
        normed = ((block - centre) * scale * gain).astype(jnp.bfloat16)
        queries += jnp.dot(normed, weight(), preferred_element_type=jnp.float32)
    return (queries * SCALE).astype(jnp.bfloat16)


def attention(place, active, queries, cache, fresh, positions):
    section, name_base = place[0], place[3]
    tokens = queries.shape[0]
    heads = queries.shape[1] // HEAD_DIM
    past = cache.shape[2]
    group = GROUP_ROWS * positions
    row_at = lax.broadcasted_iota(jnp.int32, (group, GROUP_ROWS * past), 0)
    column_at = lax.broadcasted_iota(jnp.int32, (group, GROUP_ROWS * past), 1)
    cached_mask = row_at // positions == column_at // past
    row_at = lax.broadcasted_iota(jnp.int32, (tokens, tokens), 0)
    column_at = lax.broadcasted_iota(jnp.int32, (tokens, tokens), 1)
    own_mask = (row_at // positions == column_at // positions) & (column_at <= row_at)
    transposed = (((1,), (1,)), ((), ()))
    groups = [
        (slice(at * GROUP_ROWS, (at + 1) * GROUP_ROWS), slice(at * group, (at + 1) * group))
        for at in range(tokens // group)
    ]
    lanes = [slice(head * HEAD_DIM, (head + 1) * HEAD_DIM) for head in range(heads)]
    scores = []
    for lane in lanes:
        own = lax.dot_general(
            queries[:, lane], fresh[0, :, lane], transposed, preferred_element_type=jnp.float32
        )
        cached = []
        for rows, here in groups:
            keys = cache[0, rows, :, lane].reshape(GROUP_ROWS * past, HEAD_DIM)
            score = lax.dot_general(
                queries[here, lane], keys, transposed, preferred_element_type=jnp.float32
            )
            cached.append(jnp.where(cached_mask, score, NEGATIVE))
        scores.append((jnp.where(own_mask, own, NEGATIVE), cached))
    weights = []
    for own, cached in scores:
        own_weights, cached_weights = [], []
        for score, (_, here) in zip(cached, groups):
            new = own[here]
            top = jnp.maximum(
                jnp.max(score, axis=1, keepdims=True), jnp.max(new, axis=1, keepdims=True)
            )
            score = jnp.exp(score - top)
            new = jnp.exp(new - top)
            share = 1.0 / (
                jnp.sum(score, axis=1, keepdims=True) + jnp.sum(new, axis=1, keepdims=True)
            )
            cached_weights.append((score * share).astype(jnp.bfloat16))
            own_weights.append((new * share).astype(jnp.bfloat16))
        weights.append((jnp.concatenate(own_weights, axis=0), cached_weights))
    result = []
    for head, (lane, (own, cached)) in enumerate(zip(lanes, weights)):
        mixed = jnp.dot(own, fresh[1, :, lane], preferred_element_type=jnp.float32)
        parts = []
        for weight, (rows, here) in zip(cached, groups):
            values = cache[1, rows, :, lane].reshape(GROUP_ROWS * past, HEAD_DIM)
            part = mixed[here] + jnp.dot(weight, values, preferred_element_type=jnp.float32)
            micro = rows.start // MB_ROWS
            active_now = active[micro, section, 0] == name_base + head
            for entry in range(1, active.shape[2]):
                active_now |= active[micro, section, entry] == name_base + head
            parts.append(jnp.where(active_now, part, 0.0).astype(jnp.bfloat16))
        result.append(jnp.concatenate(parts, axis=0))
    return result


def opening_kernel(
    place, active_in, inputs, gain_in, query_w, new, own_w, cache,
    kept, given_out, own_block, query_out, fresh_out, keep_w, give_w,
    active, held, gain, new_held, sems,
):
    rows, positions, model = held.shape
    tokens = rows * positions
    chip, core, chips = place[1], place[2], place[4]
    width = own_block.shape[1]
    parts = 4
    depth = model // parts
    loads = [pltpu.make_async_copy(inputs, held, sems.at[0])]
    small = [
        pltpu.make_async_copy(gain_in, gain, sems.at[parts + 3]),
        pltpu.make_async_copy(active_in, active, sems.at[parts + 4]),
    ]
    for part in range(parts):
        span = pl.ds(part * depth, depth)
        loads.append(
            pltpu.make_async_copy(query_w.at[0, span, :], query_out.at[span, :], sems.at[1 + part])
        )
    loads.append(pltpu.make_async_copy(new.at[0], new_held, sems.at[parts + 1]))
    for at, index in enumerate(ORDER):
        target = lax.rem(chip + index, chips)
        to = pl.ds(at * width, width)
        for side, held_w in ((core, keep_w), (1 - core, give_w)):
            columns = pl.ds(pl.multiple_of((2 * target + side) * width, 128), width)
            load = pltpu.make_async_copy(
                own_w.at[0, :, columns], held_w.at[:, to], sems.at[parts + 5 + len(loads)]
            )
            loads.append(load)
    for load in small + loads:
        load.start()
    loads[0].wait()
    small[0].wait()
    blocks, gains, weights = [], [], []
    for part in range(parts):
        span = slice(part * depth, (part + 1) * depth)
        blocks.append(held[:, :, span].reshape(tokens, depth).astype(jnp.float32))
        gains.append(gain[:, span])

        def weight(part=part, span=span):
            loads[1 + part].wait()
            return query_out[span, :]

        weights.append(weight)
    start = pl.multiple_of((2 * chip + core) * width, 128)
    own_block[...] = held[:, :, pl.ds(start, width)].reshape(tokens, width)
    queries = normed_queries(blocks, gains, weights)
    loads[parts + 1].wait()
    fresh_out[0] = new_held[0].reshape(tokens, fresh_out.shape[2])
    fresh_out[1] = new_held[1].reshape(tokens, fresh_out.shape[2])
    small[1].wait()
    attended = jnp.concatenate(
        attention(place, active, queries, cache, fresh_out, positions), axis=1
    )
    for load in loads[parts + 2 :]:
        load.wait()
    given = jnp.dot(attended, give_w[...], preferred_element_type=jnp.float32)
    given_out[...] = given.astype(given_out.dtype)
    kept[...] = jnp.dot(attended, keep_w[...], preferred_element_type=jnp.float32)


def give(parts, outs, current):
    if current is not None:
        parts[1] += current[...].astype(jnp.float32)
    for part, out in zip(parts, outs):
        out[...] = part.astype(out.dtype)


def merge_kernel(kept, taken, current, weights, *outs):
    del weights
    width = current.shape[1]
    for at, out in enumerate(outs[:-1]):
        here = slice(at * width, (at + 1) * width)
        part = kept[:, here] + taken[:, here].astype(jnp.float32)
        if at == len(ORDER) - 1:
            part += current[...].astype(jnp.float32)
        out[...] = part.astype(out.dtype)


def layer_kernel(positions, place, active, *refs):
    blocks = refs[:-5]
    gain, query_w, cache, fresh, out = refs[-5:]
    chip, core, chips = place[1], place[2], place[4]
    width = blocks[0].shape[1]
    values, gains, weights = [], [], []
    for at, block in enumerate(blocks):
        source = lax.rem(chip + chips - ARRIVALS[at // 2], chips)
        side = core if at % 2 == 0 else 1 - core
        span = pl.ds(pl.multiple_of((2 * source + side) * width, 128), width)
        values.append(block[...].astype(jnp.float32))
        gains.append(gain[:, span])
        weights.append(lambda span=span: query_w[span, :])
    queries = normed_queries(values, gains, weights)
    for head, mixed in enumerate(attention(place, active, queries, cache, fresh, positions)):
        out[:, head * HEAD_DIM : (head + 1) * HEAD_DIM] = mixed


def project_kernel(own, other, keep_w, take_w, *refs):
    current, outs = (None, refs) if len(refs) == 2 else (refs[0], refs[1:])
    width = outs[0].shape[1]
    first = 0 if current is None else 2
    columns = slice(first * width, (first + 2) * width)
    result = jnp.dot(own[...], keep_w[:, columns], preferred_element_type=jnp.float32)
    result += jnp.dot(other[...], take_w[:, columns], preferred_element_type=jnp.float32)
    give([result[:, :width], result[:, width:]], outs, current)


VMEM = pl.BlockSpec(memory_space=pltpu.VMEM)
SMEM = pl.BlockSpec(memory_space=pltpu.SMEM)
HBM = pl.BlockSpec(memory_space=pltpu.HBM)


def call(kernel, scalars, *args, outs, space=VMEM, scratch=(), flops=0, passed=False):
    spaces = [space] * len(args)
    out_spaces = [VMEM] * len(outs)
    aliases = {}
    if passed:
        spaces[-1] = out_spaces[-1] = pl.BlockSpec(memory_space=pl.ANY)
        aliases = {len(scalars) + len(args) - 1: len(outs) - 1}
    moved = sum(a.size * a.dtype.itemsize for a in args)
    if space is HBM:
        args = [pltpu.with_memory_space_constraint(a, pltpu.HBM) for a in args[:-1]] + [args[-1]]
        spaces[-1] = VMEM
    return pl.pallas_call(
        kernel,
        out_shape=[jax.ShapeDtypeStruct(shape, kind) for shape, kind in outs],
        in_specs=[SMEM] * len(scalars) + spaces,
        out_specs=out_spaces,
        input_output_aliases=aliases,
        scratch_shapes=scratch,
        compiler_params=pltpu.CompilerParams(vmem_limit_bytes=24 * 2**20),
        cost_estimate=pl.CostEstimate(flops=flops, bytes_accessed=moved, transcendentals=0),
    )(*scalars, *args)


def on_device(inputs, ln_gain, query_weight, out_weight, kv_cache, new_kv, active_heads):
    tensor_size = lax.axis_size("tensor")
    pipe_size = lax.axis_size("pipe")
    chips = tensor_size // 2
    section = lax.axis_index("pipe")
    slot = lax.axis_index("tensor")
    rows, positions, model = inputs.shape
    width = model // tensor_size
    tokens = rows * positions
    inner = query_weight.shape[2]
    heads = inner // HEAD_DIM
    swap = [(i, i ^ 1) for i in range(tensor_size)]
    place = jnp.stack([section, slot // 2, slot % 2, slot * heads, chips]).astype(jnp.int32)

    def across(value):
        return lax.ppermute(value, "tensor", swap)

    def send(value, by, stages):
        pairs = []
        for stage in range(pipe_size):
            for at in range(tensor_size):
                target = (stage + stages) % pipe_size * tensor_size + (at + 2 * by) % tensor_size
                pairs.append((stage * tensor_size + at, target))
        return lax.ppermute(value, ("pipe", "tensor"), pairs)

    half, full = jnp.bfloat16, jnp.float32
    chunk = ((tokens, width), half)
    kept_chunk = ((tokens, width), full)
    last_outs = [chunk, kept_chunk]
    cache = kv_cache[0]
    kept, given, current, query_w, fresh, keep_w, give_w = call(
        opening_kernel,
        (place,),
        active_heads,
        inputs,
        ln_gain,
        query_weight,
        new_kv,
        out_weight,
        cache,
        space=HBM,
        outs=[
            ((tokens, chips * width), full),
            ((tokens, chips * width), half),
            chunk,
            ((model, inner), half),
            ((2, tokens, inner), half),
            ((inner, chips * width), half),
            ((inner, chips * width), half),
        ],
        scratch=[
            pltpu.SMEM(active_heads.shape, jnp.int32),
            pltpu.VMEM((rows, positions, model), half),
            pltpu.VMEM((1, model), full),
            pltpu.VMEM((2, rows, positions, inner), half),
            pltpu.SemaphoreType.DMA((17 + 2 * chips,)),
        ],
    )
    *sent, last_chunk, own_chunk, give_w = call(
        merge_kernel,
        (),
        kept,
        across(given),
        current,
        give_w,
        outs=[chunk, chunk, chunk, kept_chunk, ((inner, chips * width), half)],
        passed=True,
    )
    last = [last_chunk, own_chunk]
    take_w = across(give_w)
    result = None
    for step in range(pipe_size):
        if step > 0:
            hopped = send(updated, 0, 1)
            arrived = {0: hopped, **{index: send(hopped, index, 0) for index in ORDER[:3]}}
            current = arrived[0]
            blocks = [b for i in ARRIVALS for b in (arrived[i], across(arrived[i]))]
            [attended] = call(
                functools.partial(layer_kernel, positions),
                (place, active_heads),
                *blocks,
                ln_gain,
                query_w,
                cache,
                fresh,
                outs=[((tokens, inner), half)],
            )
            other = across(attended)
            factors = (attended, other, keep_w, take_w)
            sent = call(project_kernel, (), *factors, outs=[chunk, chunk])
            last = call(project_kernel, (), *factors, current, outs=last_outs)
        summed = last[1]
        for index, part in zip(ORDER, (*sent, last[0])):
            summed = summed + send(part, index, 0).astype(full)
        updated = summed.astype(half)
        result = updated if result is None else jnp.where(section == step, updated, result)
    return result.reshape(1, rows, positions, width)


def solution(mesh):
    return jax.shard_map(
        on_device,
        mesh=mesh,
        in_specs=(
            P("dp", None, None),
            P("pipe", None),
            P("pipe", None, "tensor"),
            P("pipe", "tensor", None),
            P("pipe", None, "dp", None, "tensor"),
            P("pipe", None, "dp", None, "tensor"),
            P("dp", None, None),
        ),
        out_specs=P("pipe", "dp", None, "tensor"),
        check_vma=False,
    )
```

```python
import functools

import jax
import jax.numpy as jnp
from jax import lax
from jax.experimental import pallas as pl
from jax.experimental.pallas import tpu as pltpu
from jax.sharding import PartitionSpec as P

HEAD_DIM = 128
MB_ROWS = 8
NEGATIVE = -1e30
EPSILON = 1e-05
SCALE = HEAD_DIM ** (-0.5)
ORDER = (2, 1, 3, 0)
ARRIVALS = (0, 2, 1, 3)
GROUP_ROWS = 4


def normed_queries(blocks, gains, weights):
    tokens = blocks[0].shape[0]
    model = sum(block.shape[1] for block in blocks)
    total = jnp.zeros((tokens, 1), jnp.float32)
    for block in blocks:
        total += jnp.sum(block, axis=1, keepdims=True)
    centre = total / model
    total = jnp.zeros((tokens, 1), jnp.float32)
    for block in blocks:
        total += jnp.sum(jnp.square(block - centre), axis=1, keepdims=True)
    scale = lax.rsqrt(total / model + EPSILON)
    queries = 0.0
    for block, gain, weight in zip(blocks, gains, weights):
        normed = ((block - centre) * scale * gain).astype(jnp.bfloat16)
        queries += jnp.dot(normed, weight(), preferred_element_type=jnp.float32)
    return (queries * SCALE).astype(jnp.bfloat16)


def attention(place, active, queries, cache, fresh, positions):
    section, name_base = place[0], place[3]
    tokens = queries.shape[0]
    heads = queries.shape[1] // HEAD_DIM
    past = cache.shape[2]
    group = GROUP_ROWS * positions
    row_at = lax.broadcasted_iota(jnp.int32, (group, GROUP_ROWS * past), 0)
    column_at = lax.broadcasted_iota(jnp.int32, (group, GROUP_ROWS * past), 1)
    cached_mask = row_at // positions == column_at // past
    row_at = lax.broadcasted_iota(jnp.int32, (tokens, tokens), 0)
    column_at = lax.broadcasted_iota(jnp.int32, (tokens, tokens), 1)
    own_mask = (row_at // positions == column_at // positions) & (column_at <= row_at)
    transposed = (((1,), (1,)), ((), ()))
    groups = [
        (slice(at * GROUP_ROWS, (at + 1) * GROUP_ROWS), slice(at * group, (at + 1) * group))
        for at in range(tokens // group)
    ]
    lanes = [slice(head * HEAD_DIM, (head + 1) * HEAD_DIM) for head in range(heads)]
    scores = []
    for lane in lanes:
        own = lax.dot_general(
            queries[:, lane], fresh[0, :, lane], transposed, preferred_element_type=jnp.float32
        )
        cached = []
        for rows, here in groups:
            keys = cache[0, rows, :, lane].reshape(GROUP_ROWS * past, HEAD_DIM)
            score = lax.dot_general(
                queries[here, lane], keys, transposed, preferred_element_type=jnp.float32
            )
            cached.append(jnp.where(cached_mask, score, NEGATIVE))
        scores.append((jnp.where(own_mask, own, NEGATIVE), cached))
    weights = []
    for own, cached in scores:
        own_weights, cached_weights = [], []
        for score, (_, here) in zip(cached, groups):
            new = own[here]
            top = jnp.maximum(
                jnp.max(score, axis=1, keepdims=True), jnp.max(new, axis=1, keepdims=True)
            )
            score = jnp.exp(score - top)
            new = jnp.exp(new - top)
            share = 1.0 / (
                jnp.sum(score, axis=1, keepdims=True) + jnp.sum(new, axis=1, keepdims=True)
            )
            cached_weights.append((score * share).astype(jnp.bfloat16))
            own_weights.append((new * share).astype(jnp.bfloat16))
        weights.append((jnp.concatenate(own_weights, axis=0), cached_weights))
    result = []
    for head, (lane, (own, cached)) in enumerate(zip(lanes, weights)):
        mixed = jnp.dot(own, fresh[1, :, lane], preferred_element_type=jnp.float32)
        parts = []
        for weight, (rows, here) in zip(cached, groups):
            values = cache[1, rows, :, lane].reshape(GROUP_ROWS * past, HEAD_DIM)
            part = mixed[here] + jnp.dot(weight, values, preferred_element_type=jnp.float32)
            micro = rows.start // MB_ROWS
            active_now = active[micro, section, 0] == name_base + head
            for entry in range(1, active.shape[2]):
                active_now |= active[micro, section, entry] == name_base + head
            parts.append(jnp.where(active_now, part, 0.0).astype(jnp.bfloat16))
        result.append(jnp.concatenate(parts, axis=0))
    return result


def first_queries_kernel(place, inputs, gain, query_w, queries, own_block):
    rows, positions, model = inputs.shape
    tokens = rows * positions
    width = own_block.shape[1]
    depth = model // 4
    blocks, gains, weights = [], [], []
    for start in range(0, model, depth):
        span = slice(start, start + depth)
        blocks.append(inputs[:, :, span].reshape(tokens, depth).astype(jnp.float32))
        gains.append(gain[:, span])
        weights.append(lambda span=span: query_w[span, :])
    start = pl.multiple_of((2 * place[1] + place[2]) * width, 128)
    own_block[...] = inputs[:, :, pl.ds(start, width)].reshape(tokens, width)
    queries[...] = normed_queries(blocks, gains, weights)


def first_attend_kernel(place, active, queries, cache, new, out, fresh):
    tokens, inner = queries.shape
    for part in range(2):
        fresh[part] = new[part].reshape(tokens, inner)
    positions = new.shape[2]
    heads = attention(place, active, queries[...], cache, fresh, positions)
    for head, mixed in enumerate(heads):
        out[:, head * HEAD_DIM : (head + 1) * HEAD_DIM] = mixed


def first_project_kernel(place, attended, own_w, kept, given, keep_w, give_w):
    chip, core, chips = place[1], place[2], place[4]
    width = kept.shape[1] // len(ORDER)
    for at, index in enumerate(ORDER):
        target = lax.rem(chip + index, chips)
        to = slice(at * width, (at + 1) * width)
        for side, packed in ((core, keep_w), (1 - core, give_w)):
            columns = pl.ds(pl.multiple_of((2 * target + side) * width, 128), width)
            packed[:, to] = own_w[:, columns]
    result = jnp.dot(attended[...], give_w[...], preferred_element_type=jnp.float32)
    given[...] = result.astype(given.dtype)
    kept[...] = jnp.dot(attended[...], keep_w[...], preferred_element_type=jnp.float32)


def give(parts, outs, current):
    if current is not None:
        parts[1] += current[...].astype(jnp.float32)
    for part, out in zip(parts, outs):
        out[...] = part.astype(out.dtype)


def merge_kernel(kept, taken, current, weights, *outs):
    del weights
    width = current.shape[1]
    for at, out in enumerate(outs[:-1]):
        here = slice(at * width, (at + 1) * width)
        part = kept[:, here] + taken[:, here].astype(jnp.float32)
        if at == len(ORDER) - 1:
            part += current[...].astype(jnp.float32)
        out[...] = part.astype(out.dtype)


def layer_kernel(positions, place, active, *refs):
    blocks = refs[:-5]
    gain, query_w, cache, fresh, out = refs[-5:]
    chip, core, chips = place[1], place[2], place[4]
    width = blocks[0].shape[1]
    values, gains, weights = [], [], []
    for at, block in enumerate(blocks):
        source = lax.rem(chip + chips - ARRIVALS[at // 2], chips)
        side = core if at % 2 == 0 else 1 - core
        span = pl.ds(pl.multiple_of((2 * source + side) * width, 128), width)
        values.append(block[...].astype(jnp.float32))
        gains.append(gain[:, span])
        weights.append(lambda span=span: query_w[span, :])
    queries = normed_queries(values, gains, weights)
    for head, mixed in enumerate(attention(place, active, queries, cache, fresh, positions)):
        out[:, head * HEAD_DIM : (head + 1) * HEAD_DIM] = mixed


def project_kernel(own, other, keep_w, take_w, *refs):
    current, outs = (None, refs) if len(refs) == 2 else (refs[0], refs[1:])
    width = outs[0].shape[1]
    first = 0 if current is None else 2
    columns = slice(first * width, (first + 2) * width)
    result = jnp.dot(own[...], keep_w[:, columns], preferred_element_type=jnp.float32)
    result += jnp.dot(other[...], take_w[:, columns], preferred_element_type=jnp.float32)
    give([result[:, :width], result[:, width:]], outs, current)


VMEM = pl.BlockSpec(memory_space=pltpu.VMEM)
SMEM = pl.BlockSpec(memory_space=pltpu.SMEM)


def call(kernel, scalars, *args, outs, passed=False):
    spaces = [VMEM] * len(args)
    out_spaces = [VMEM] * len(outs)
    aliases = {}
    if passed:
        spaces[-1] = out_spaces[-1] = pl.BlockSpec(memory_space=pl.ANY)
        aliases = {len(scalars) + len(args) - 1: len(outs) - 1}
    moved = sum(a.size * a.dtype.itemsize for a in args)
    return pl.pallas_call(
        kernel,
        out_shape=[jax.ShapeDtypeStruct(shape, kind) for shape, kind in outs],
        in_specs=[SMEM] * len(scalars) + spaces,
        out_specs=out_spaces,
        input_output_aliases=aliases,
        compiler_params=pltpu.CompilerParams(vmem_limit_bytes=24 * 2**20),
        cost_estimate=pl.CostEstimate(flops=0, bytes_accessed=moved, transcendentals=0),
    )(*scalars, *args)


def on_device(inputs, ln_gain, query_weight, out_weight, kv_cache, new_kv, active_heads):
    tensor_size = lax.axis_size("tensor")
    pipe_size = lax.axis_size("pipe")
    chips = tensor_size // 2
    section = lax.axis_index("pipe")
    slot = lax.axis_index("tensor")
    rows, positions, model = inputs.shape
    width = model // tensor_size
    tokens = rows * positions
    inner = query_weight.shape[2]
    heads = inner // HEAD_DIM
    swap = [(i, i ^ 1) for i in range(tensor_size)]
    place = jnp.stack([section, slot // 2, slot % 2, slot * heads, chips]).astype(jnp.int32)

    def across(value):
        return lax.ppermute(value, "tensor", swap)

    def send(value, by, stages):
        pairs = []
        for stage in range(pipe_size):
            for at in range(tensor_size):
                target = (stage + stages) % pipe_size * tensor_size + (at + 2 * by) % tensor_size
                pairs.append((stage * tensor_size + at, target))
        return lax.ppermute(value, ("pipe", "tensor"), pairs)

    half, full = jnp.bfloat16, jnp.float32
    chunk = ((tokens, width), half)
    kept_chunk = ((tokens, width), full)
    last_outs = [chunk, kept_chunk]
    query_w, cache = query_weight[0], kv_cache[0]
    head_shape = ((tokens, inner), half)
    packed_shape = ((inner, chips * width), half)
    queries, current = call(
        first_queries_kernel, (place,), inputs, ln_gain, query_w, outs=[head_shape, chunk]
    )
    attended, fresh = call(
        first_attend_kernel,
        (place, active_heads),
        queries,
        cache,
        new_kv[0],
        outs=[head_shape, ((2, tokens, inner), half)],
    )
    kept, given, keep_w, give_w = call(
        first_project_kernel,
        (place,),
        attended,
        out_weight[0],
        outs=[
            ((tokens, chips * width), full),
            ((tokens, chips * width), half),
            packed_shape,
            packed_shape,
        ],
    )
    *sent, last_chunk, own_chunk, give_w = call(
        merge_kernel,
        (),
        kept,
        across(given),
        current,
        give_w,
        outs=[chunk, chunk, chunk, kept_chunk, ((inner, chips * width), half)],
        passed=True,
    )
    last = [last_chunk, own_chunk]
    take_w = across(give_w)
    result = None
    for step in range(pipe_size):
        if step > 0:
            hopped = send(updated, 0, 1)
            arrived = {0: hopped, **{index: send(hopped, index, 0) for index in ORDER[:3]}}
            current = arrived[0]
            blocks = [b for i in ARRIVALS for b in (arrived[i], across(arrived[i]))]
            [attended] = call(
                functools.partial(layer_kernel, positions),
                (place, active_heads),
                *blocks,
                ln_gain,
                query_w,
                cache,
                fresh,
                outs=[((tokens, inner), half)],
            )
            other = across(attended)
            factors = (attended, other, keep_w, take_w)
            sent = call(project_kernel, (), *factors, outs=[chunk, chunk])
            last = call(project_kernel, (), *factors, current, outs=last_outs)
        summed = last[1]
        for index, part in zip(ORDER, (*sent, last[0])):
            summed = summed + send(part, index, 0).astype(full)
        updated = summed.astype(half)
        result = updated if result is None else jnp.where(section == step, updated, result)
    return result.reshape(1, rows, positions, width)


def solution(mesh):
    return jax.shard_map(
        on_device,
        mesh=mesh,
        in_specs=(
            P("dp", None, None),
            P("pipe", None),
            P("pipe", None, "tensor"),
            P("pipe", "tensor", None),
            P("pipe", None, "dp", None, "tensor"),
            P("pipe", None, "dp", None, "tensor"),
            P("dp", None, None),
        ),
        out_specs=P("pipe", "dp", None, "tensor"),
        check_vma=False,
    )
```

```python
import functools

import jax
import jax.numpy as jnp
from jax import lax
from jax.experimental import pallas as pl
from jax.experimental.pallas import tpu as pltpu
from jax.sharding import PartitionSpec as P

HEAD_DIM = 128
MB_ROWS = 8
NEGATIVE = -1e30
EPSILON = 1e-05
SCALE = HEAD_DIM ** (-0.5)
ORDER = (2, 1, 3, 0)
ARRIVALS = (0, 2, 1, 3)
GROUP_ROWS = 4


def normed_queries(blocks, gains, weights):
    tokens = blocks[0].shape[0]
    model = sum(block.shape[1] for block in blocks)
    total = jnp.zeros((tokens, 1), jnp.float32)
    for block in blocks:
        total += jnp.sum(block, axis=1, keepdims=True)
    centre = total / model
    total = jnp.zeros((tokens, 1), jnp.float32)
    for block in blocks:
        total += jnp.sum(jnp.square(block - centre), axis=1, keepdims=True)
    scale = lax.rsqrt(total / model + EPSILON)
    queries = 0.0
    for block, gain, weight in zip(blocks, gains, weights):
        normed = ((block - centre) * scale * gain).astype(jnp.bfloat16)
        queries += jnp.dot(normed, weight(), preferred_element_type=jnp.float32)
    return (queries * SCALE).astype(jnp.bfloat16)


def attention(place, active, queries, cache, fresh, positions):
    section, name_base = place[0], place[3]
    tokens = queries.shape[0]
    heads = queries.shape[1] // HEAD_DIM
    past = cache.shape[2]
    group = GROUP_ROWS * positions
    row_at = lax.broadcasted_iota(jnp.int32, (group, GROUP_ROWS * past), 0)
    column_at = lax.broadcasted_iota(jnp.int32, (group, GROUP_ROWS * past), 1)
    cached_mask = row_at // positions == column_at // past
    row_at = lax.broadcasted_iota(jnp.int32, (tokens, tokens), 0)
    column_at = lax.broadcasted_iota(jnp.int32, (tokens, tokens), 1)
    own_mask = (row_at // positions == column_at // positions) & (column_at <= row_at)
    transposed = (((1,), (1,)), ((), ()))
    groups = [
        (slice(at * GROUP_ROWS, (at + 1) * GROUP_ROWS), slice(at * group, (at + 1) * group))
        for at in range(tokens // group)
    ]
    lanes = [slice(head * HEAD_DIM, (head + 1) * HEAD_DIM) for head in range(heads)]
    scores = []
    for lane in lanes:
        own = lax.dot_general(
            queries[:, lane], fresh[0, :, lane], transposed, preferred_element_type=jnp.float32
        )
        cached = []
        for rows, here in groups:
            keys = cache[0, rows, :, lane].reshape(GROUP_ROWS * past, HEAD_DIM)
            score = lax.dot_general(
                queries[here, lane], keys, transposed, preferred_element_type=jnp.float32
            )
            cached.append(jnp.where(cached_mask, score, NEGATIVE))
        scores.append((jnp.where(own_mask, own, NEGATIVE), cached))
    weights = []
    for own, cached in scores:
        own_weights, cached_weights = [], []
        for score, (_, here) in zip(cached, groups):
            new = own[here]
            top = jnp.maximum(
                jnp.max(score, axis=1, keepdims=True), jnp.max(new, axis=1, keepdims=True)
            )
            score = jnp.exp(score - top)
            new = jnp.exp(new - top)
            share = 1.0 / (
                jnp.sum(score, axis=1, keepdims=True) + jnp.sum(new, axis=1, keepdims=True)
            )
            cached_weights.append((score * share).astype(jnp.bfloat16))
            own_weights.append((new * share).astype(jnp.bfloat16))
        weights.append((jnp.concatenate(own_weights, axis=0), cached_weights))
    result = []
    for head, (lane, (own, cached)) in enumerate(zip(lanes, weights)):
        mixed = jnp.dot(own, fresh[1, :, lane], preferred_element_type=jnp.float32)
        parts = []
        for weight, (rows, here) in zip(cached, groups):
            values = cache[1, rows, :, lane].reshape(GROUP_ROWS * past, HEAD_DIM)
            part = mixed[here] + jnp.dot(weight, values, preferred_element_type=jnp.float32)
            micro = rows.start // MB_ROWS
            active_now = active[micro, section, 0] == name_base + head
            for entry in range(1, active.shape[2]):
                active_now |= active[micro, section, entry] == name_base + head
            parts.append(jnp.where(active_now, part, 0.0).astype(jnp.bfloat16))
        result.append(jnp.concatenate(parts, axis=0))
    return result


def opening_kernel(
    place, active_in, inputs, gain_in, query_w, cache, new, own_w,
    kept, given_out, own_block, query_out, cache_out, fresh_out, keep_w, give_w,
    active, held, gain, new_held, sems,
):
    rows, positions, model = held.shape
    tokens = rows * positions
    chip, core, chips = place[1], place[2], place[4]
    width = own_block.shape[1]
    parts = 4
    depth = model // parts
    loads = [pltpu.make_async_copy(inputs, held, sems.at[0])]
    small = [
        pltpu.make_async_copy(gain_in, gain, sems.at[parts + 3]),
        pltpu.make_async_copy(active_in, active, sems.at[parts + 4]),
    ]
    for part in range(parts):
        span = pl.ds(part * depth, depth)
        loads.append(
            pltpu.make_async_copy(query_w.at[0, span, :], query_out.at[span, :], sems.at[1 + part])
        )
    loads.append(pltpu.make_async_copy(new.at[0], new_held, sems.at[parts + 1]))
    loads.append(pltpu.make_async_copy(cache.at[0], cache_out, sems.at[parts + 2]))
    for at, index in enumerate(ORDER):
        target = lax.rem(chip + index, chips)
        to = pl.ds(at * width, width)
        for side, held_w in ((core, keep_w), (1 - core, give_w)):
            columns = pl.ds(pl.multiple_of((2 * target + side) * width, 128), width)
            load = pltpu.make_async_copy(
                own_w.at[0, :, columns], held_w.at[:, to], sems.at[parts + 5 + len(loads)]
            )
            loads.append(load)
    for load in small + loads:
        load.start()
    loads[0].wait()
    small[0].wait()
    blocks, gains, weights = [], [], []
    for part in range(parts):
        span = slice(part * depth, (part + 1) * depth)
        blocks.append(held[:, :, span].reshape(tokens, depth).astype(jnp.float32))
        gains.append(gain[:, span])

        def weight(part=part, span=span):
            loads[1 + part].wait()
            return query_out[span, :]

        weights.append(weight)
    start = pl.multiple_of((2 * chip + core) * width, 128)
    own_block[...] = held[:, :, pl.ds(start, width)].reshape(tokens, width)
    queries = normed_queries(blocks, gains, weights)
    loads[parts + 1].wait()
    fresh_out[0] = new_held[0].reshape(tokens, fresh_out.shape[2])
    fresh_out[1] = new_held[1].reshape(tokens, fresh_out.shape[2])
    loads[parts + 2].wait()
    small[1].wait()
    attended = jnp.concatenate(
        attention(place, active, queries, cache_out, fresh_out, positions), axis=1
    )
    for load in loads[parts + 3 :]:
        load.wait()
    given = jnp.dot(attended, give_w[...], preferred_element_type=jnp.float32)
    given_out[...] = given.astype(given_out.dtype)
    kept[...] = jnp.dot(attended, keep_w[...], preferred_element_type=jnp.float32)


def give(parts, outs, current):
    if current is not None:
        parts[1] += current[...].astype(jnp.float32)
    for part, out in zip(parts, outs):
        out[...] = part.astype(out.dtype)


def merge_kernel(kept, taken, current, weights, *outs):
    del weights
    width = current.shape[1]
    for at, out in enumerate(outs[:-1]):
        here = slice(at * width, (at + 1) * width)
        part = kept[:, here] + taken[:, here].astype(jnp.float32)
        if at == len(ORDER) - 1:
            part += current[...].astype(jnp.float32)
        out[...] = part.astype(out.dtype)


def layer_kernel(positions, place, active, *refs):
    blocks = refs[:-5]
    gain, query_w, cache, fresh, out = refs[-5:]
    chip, core, chips = place[1], place[2], place[4]
    width = blocks[0].shape[1]
    values, gains, weights = [], [], []
    for at, block in enumerate(blocks):
        source = lax.rem(chip + chips - ARRIVALS[at // 2], chips)
        side = core if at % 2 == 0 else 1 - core
        span = pl.ds(pl.multiple_of((2 * source + side) * width, 128), width)
        values.append(block[...].astype(jnp.float32))
        gains.append(gain[:, span])
        weights.append(lambda span=span: query_w[span, :])
    queries = normed_queries(values, gains, weights)
    for head, mixed in enumerate(attention(place, active, queries, cache, fresh, positions)):
        out[:, head * HEAD_DIM : (head + 1) * HEAD_DIM] = mixed


def project_kernel(own, other, keep_w, take_w, *refs):
    current, outs = (None, refs) if len(refs) == 2 else (refs[0], refs[1:])
    width = outs[0].shape[1]
    first = 0 if current is None else 2
    columns = slice(first * width, (first + 2) * width)
    result = jnp.dot(own[...], keep_w[:, columns], preferred_element_type=jnp.float32)
    result += jnp.dot(other[...], take_w[:, columns], preferred_element_type=jnp.float32)
    give([result[:, :width], result[:, width:]], outs, current)


VMEM = pl.BlockSpec(memory_space=pltpu.VMEM)
SMEM = pl.BlockSpec(memory_space=pltpu.SMEM)
HBM = pl.BlockSpec(memory_space=pltpu.HBM)


def call(kernel, scalars, *args, outs, space=VMEM, scratch=(), flops=0, passed=False):
    spaces = [space] * len(args)
    out_spaces = [VMEM] * len(outs)
    aliases = {}
    if passed:
        spaces[-1] = out_spaces[-1] = pl.BlockSpec(memory_space=pl.ANY)
        aliases = {len(scalars) + len(args) - 1: len(outs) - 1}
    moved = sum(a.size * a.dtype.itemsize for a in args)
    if space is HBM:
        args = [pltpu.with_memory_space_constraint(a, pltpu.HBM) for a in args]
    return pl.pallas_call(
        kernel,
        out_shape=[jax.ShapeDtypeStruct(shape, kind) for shape, kind in outs],
        in_specs=[SMEM] * len(scalars) + spaces,
        out_specs=out_spaces,
        input_output_aliases=aliases,
        scratch_shapes=scratch,
        compiler_params=pltpu.CompilerParams(vmem_limit_bytes=24 * 2**20),
        cost_estimate=pl.CostEstimate(flops=flops, bytes_accessed=moved, transcendentals=0),
    )(*scalars, *args)


def on_device(inputs, ln_gain, query_weight, out_weight, kv_cache, new_kv, active_heads):
    tensor_size = lax.axis_size("tensor")
    pipe_size = lax.axis_size("pipe")
    chips = tensor_size // 2
    section = lax.axis_index("pipe")
    slot = lax.axis_index("tensor")
    rows, positions, model = inputs.shape
    width = model // tensor_size
    tokens = rows * positions
    inner = query_weight.shape[2]
    heads = inner // HEAD_DIM
    past = kv_cache.shape[3]
    swap = [(i, i ^ 1) for i in range(tensor_size)]
    place = jnp.stack([section, slot // 2, slot % 2, slot * heads, chips]).astype(jnp.int32)

    def across(value):
        return lax.ppermute(value, "tensor", swap)

    def send(value, by, stages):
        pairs = []
        for stage in range(pipe_size - stages):
            for at in range(tensor_size):
                target = (stage + stages) * tensor_size + (at + 2 * by) % tensor_size
                pairs.append((stage * tensor_size + at, target))
        return lax.ppermute(value, ("pipe", "tensor"), pairs)

    half, full = jnp.bfloat16, jnp.float32
    chunk = ((tokens, width), half)
    kept_chunk = ((tokens, width), full)
    last_outs = [chunk, kept_chunk]
    kept, given, current, query_w, cache, fresh, keep_w, give_w = call(
        opening_kernel,
        (place,),
        active_heads,
        inputs,
        ln_gain,
        query_weight,
        kv_cache,
        new_kv,
        out_weight,
        space=HBM,
        outs=[
            ((tokens, chips * width), full),
            ((tokens, chips * width), half),
            chunk,
            ((model, inner), half),
            ((2, rows, past, inner), half),
            ((2, tokens, inner), half),
            ((inner, chips * width), half),
            ((inner, chips * width), half),
        ],
        scratch=[
            pltpu.SMEM(active_heads.shape, jnp.int32),
            pltpu.VMEM((rows, positions, model), half),
            pltpu.VMEM((1, model), full),
            pltpu.VMEM((2, rows, positions, inner), half),
            pltpu.SemaphoreType.DMA((17 + 2 * chips,)),
        ],
    )
    *sent, last_chunk, own_chunk, give_w = call(
        merge_kernel,
        (),
        kept,
        across(given),
        current,
        give_w,
        outs=[chunk, chunk, chunk, kept_chunk, ((inner, chips * width), half)],
        passed=True,
    )
    last = [last_chunk, own_chunk]
    take_w = across(give_w)
    result = None
    for step in range(pipe_size):
        if step > 0:
            hopped = send(updated, 0, 1)
            arrived = {0: hopped, **{index: send(hopped, index, 0) for index in ORDER[:3]}}
            current = arrived[0]
            blocks = [b for i in ARRIVALS for b in (arrived[i], across(arrived[i]))]
            [attended] = call(
                functools.partial(layer_kernel, positions),
                (place, active_heads),
                *blocks,
                ln_gain,
                query_w,
                cache,
                fresh,
                outs=[((tokens, inner), half)],
            )
            other = across(attended)
            factors = (attended, other, keep_w, take_w)
            sent = call(project_kernel, (), *factors, outs=[chunk, chunk])
            last = call(project_kernel, (), *factors, current, outs=last_outs)
        summed = last[1]
        for index, part in zip(ORDER, (*sent, last[0])):
            summed = summed + send(part, index, 0).astype(full)
        updated = summed.astype(half)
        result = updated if result is None else jnp.where(section == step, updated, result)
    return result.reshape(1, rows, positions, width)


def solution(mesh):
    return jax.shard_map(
        on_device,
        mesh=mesh,
        in_specs=(
            P("dp", None, None),
            P("pipe", None),
            P("pipe", None, "tensor"),
            P("pipe", "tensor", None),
            P("pipe", None, "dp", None, "tensor"),
            P("pipe", None, "dp", None, "tensor"),
            P("dp", None, None),
        ),
        out_specs=P("pipe", "dp", None, "tensor"),
        check_vma=False,
    )
```

```python
import functools

import jax
import jax.numpy as jnp
from jax import lax
from jax.experimental import pallas as pl
from jax.experimental.pallas import tpu as pltpu
from jax.sharding import PartitionSpec as P

HEAD_DIM = 128
MB_ROWS = 8
NEGATIVE = -1e30
EPSILON = 1e-05
SCALE = HEAD_DIM ** (-0.5)
ORDER = (2, 1, 3, 0)
ARRIVALS = (0, 2, 1, 3)
GROUP_ROWS = 4


def normed_queries(blocks, gains, weights):
    tokens = blocks[0].shape[0]
    model = sum(block.shape[1] for block in blocks)
    total = jnp.zeros((tokens, 1), jnp.float32)
    for block in blocks:
        total += jnp.sum(block, axis=1, keepdims=True)
    centre = total / model
    total = jnp.zeros((tokens, 1), jnp.float32)
    for block in blocks:
        total += jnp.sum(jnp.square(block - centre), axis=1, keepdims=True)
    scale = lax.rsqrt(total / model + EPSILON)
    queries = 0.0
    for block, gain, weight in zip(blocks, gains, weights):
        normed = ((block - centre) * scale * gain).astype(jnp.bfloat16)
        queries += jnp.dot(normed, weight(), preferred_element_type=jnp.float32)
    return (queries * SCALE).astype(jnp.bfloat16)


def attention(place, active, queries, cache, fresh, positions):
    section, name_base = place[0], place[3]
    tokens = queries.shape[0]
    heads = queries.shape[1] // HEAD_DIM
    past = cache.shape[2]
    group = GROUP_ROWS * positions
    row_at = lax.broadcasted_iota(jnp.int32, (group, GROUP_ROWS * past), 0)
    column_at = lax.broadcasted_iota(jnp.int32, (group, GROUP_ROWS * past), 1)
    cached_mask = row_at // positions == column_at // past
    row_at = lax.broadcasted_iota(jnp.int32, (tokens, tokens), 0)
    column_at = lax.broadcasted_iota(jnp.int32, (tokens, tokens), 1)
    own_mask = (row_at // positions == column_at // positions) & (column_at <= row_at)
    transposed = (((1,), (1,)), ((), ()))
    groups = [
        (slice(at * GROUP_ROWS, (at + 1) * GROUP_ROWS), slice(at * group, (at + 1) * group))
        for at in range(tokens // group)
    ]
    lanes = [slice(head * HEAD_DIM, (head + 1) * HEAD_DIM) for head in range(heads)]
    scores = []
    for lane in lanes:
        own = lax.dot_general(
            queries[:, lane], fresh[0, :, lane], transposed, preferred_element_type=jnp.float32
        )
        cached = []
        for rows, here in groups:
            keys = cache[0, rows, :, lane].reshape(GROUP_ROWS * past, HEAD_DIM)
            score = lax.dot_general(
                queries[here, lane], keys, transposed, preferred_element_type=jnp.float32
            )
            cached.append(jnp.where(cached_mask, score, NEGATIVE))
        scores.append((jnp.where(own_mask, own, NEGATIVE), cached))
    weights = []
    for own, cached in scores:
        own_weights, cached_weights = [], []
        for score, (_, here) in zip(cached, groups):
            new = own[here]
            top = jnp.maximum(
                jnp.max(score, axis=1, keepdims=True), jnp.max(new, axis=1, keepdims=True)
            )
            score = jnp.exp(score - top)
            new = jnp.exp(new - top)
            share = 1.0 / (
                jnp.sum(score, axis=1, keepdims=True) + jnp.sum(new, axis=1, keepdims=True)
            )
            cached_weights.append((score * share).astype(jnp.bfloat16))
            own_weights.append((new * share).astype(jnp.bfloat16))
        weights.append((jnp.concatenate(own_weights, axis=0), cached_weights))
    result = []
    for head, (lane, (own, cached)) in enumerate(zip(lanes, weights)):
        mixed = jnp.dot(own, fresh[1, :, lane], preferred_element_type=jnp.float32)
        parts = []
        for weight, (rows, here) in zip(cached, groups):
            values = cache[1, rows, :, lane].reshape(GROUP_ROWS * past, HEAD_DIM)
            part = mixed[here] + jnp.dot(weight, values, preferred_element_type=jnp.float32)
            micro = rows.start // MB_ROWS
            active_now = active[micro, section, 0] == name_base + head
            for entry in range(1, active.shape[2]):
                active_now |= active[micro, section, entry] == name_base + head
            parts.append(jnp.where(active_now, part, 0.0).astype(jnp.bfloat16))
        result.append(jnp.concatenate(parts, axis=0))
    return result


def opening_kernel(
    place, active_in, inputs, gain_in, query_w, cache, new, own_w,
    kept, given_out, own_block, query_out, cache_out, fresh_out, keep_w, give_w,
    active, held, gain, new_held, sems,
):
    rows, positions, model = held.shape
    tokens = rows * positions
    chip, core, chips = place[1], place[2], place[4]
    width = own_block.shape[1]
    parts = 4
    depth = model // parts
    loads = [pltpu.make_async_copy(inputs, held, sems.at[0])]
    small = [
        pltpu.make_async_copy(gain_in, gain, sems.at[parts + 3]),
        pltpu.make_async_copy(active_in, active, sems.at[parts + 4]),
    ]
    for part in range(parts):
        span = pl.ds(part * depth, depth)
        loads.append(
            pltpu.make_async_copy(query_w.at[0, span, :], query_out.at[span, :], sems.at[1 + part])
        )
    loads.append(pltpu.make_async_copy(new.at[0], new_held, sems.at[parts + 1]))
    loads.append(pltpu.make_async_copy(cache.at[0], cache_out, sems.at[parts + 2]))
    for at, index in enumerate(ORDER):
        target = lax.rem(chip + index, chips)
        to = pl.ds(at * width, width)
        for side, held_w in ((core, keep_w), (1 - core, give_w)):
            columns = pl.ds(pl.multiple_of((2 * target + side) * width, 128), width)
            load = pltpu.make_async_copy(
                own_w.at[0, :, columns], held_w.at[:, to], sems.at[parts + 5 + len(loads)]
            )
            loads.append(load)
    for load in small + loads:
        load.start()
    loads[0].wait()
    small[0].wait()
    blocks, gains, weights = [], [], []
    for part in range(parts):
        span = slice(part * depth, (part + 1) * depth)
        blocks.append(held[:, :, span].reshape(tokens, depth).astype(jnp.float32))
        gains.append(gain[:, span])

        def weight(part=part, span=span):
            loads[1 + part].wait()
            return query_out[span, :]

        weights.append(weight)
    start = pl.multiple_of((2 * chip + core) * width, 128)
    own_block[...] = held[:, :, pl.ds(start, width)].reshape(tokens, width)
    queries = normed_queries(blocks, gains, weights)
    loads[parts + 1].wait()
    fresh_out[0] = new_held[0].reshape(tokens, fresh_out.shape[2])
    fresh_out[1] = new_held[1].reshape(tokens, fresh_out.shape[2])
    loads[parts + 2].wait()
    small[1].wait()
    attended = jnp.concatenate(
        attention(place, active, queries, cache_out, fresh_out, positions), axis=1
    )
    for load in loads[parts + 3 :]:
        load.wait()
    given = jnp.dot(attended, give_w[...], preferred_element_type=jnp.float32)
    given_out[...] = given.astype(given_out.dtype)
    kept[...] = jnp.dot(attended, keep_w[...], preferred_element_type=jnp.float32)


def give(parts, outs, current):
    if current is not None:
        parts[1] += current[...].astype(jnp.float32)
    for part, out in zip(parts, outs):
        out[...] = part.astype(out.dtype)


def merge_kernel(kept, taken, current, weights, *outs):
    del weights
    width = current.shape[1]
    for at, out in enumerate(outs[:-1]):
        here = slice(at * width, (at + 1) * width)
        part = kept[:, here] + taken[:, here].astype(jnp.float32)
        if at == len(ORDER) - 1:
            part += current[...].astype(jnp.float32)
        out[...] = part.astype(out.dtype)


def layer_kernel(positions, place, active, *refs):
    blocks = refs[:-5]
    gain, query_w, cache, fresh, out = refs[-5:]
    chip, core, chips = place[1], place[2], place[4]
    width = blocks[0].shape[1]
    values, gains, weights = [], [], []
    for at, block in enumerate(blocks):
        source = lax.rem(chip + chips - ARRIVALS[at // 2], chips)
        side = core if at % 2 == 0 else 1 - core
        span = pl.ds(pl.multiple_of((2 * source + side) * width, 128), width)
        values.append(block[...].astype(jnp.float32))
        gains.append(gain[:, span])
        weights.append(lambda span=span: query_w[span, :])
    queries = normed_queries(values, gains, weights)
    for head, mixed in enumerate(attention(place, active, queries, cache, fresh, positions)):
        out[:, head * HEAD_DIM : (head + 1) * HEAD_DIM] = mixed


def project_kernel(own, other, keep_w, take_w, *refs):
    current, outs = (None, refs) if len(refs) == 2 else (refs[0], refs[1:])
    width = outs[0].shape[1]
    first = 0 if current is None else 2
    columns = slice(first * width, (first + 2) * width)
    result = jnp.dot(own[...], keep_w[:, columns], preferred_element_type=jnp.float32)
    result += jnp.dot(other[...], take_w[:, columns], preferred_element_type=jnp.float32)
    give([result[:, :width], result[:, width:]], outs, current)


VMEM = pl.BlockSpec(memory_space=pltpu.VMEM)
SMEM = pl.BlockSpec(memory_space=pltpu.SMEM)
HBM = pl.BlockSpec(memory_space=pltpu.HBM)


def call(kernel, scalars, *args, outs, space=VMEM, scratch=(), flops=0, passed=False):
    spaces = [space] * len(args)
    out_spaces = [VMEM] * len(outs)
    aliases = {}
    if passed:
        spaces[-1] = out_spaces[-1] = pl.BlockSpec(memory_space=pl.ANY)
        aliases = {len(scalars) + len(args) - 1: len(outs) - 1}
    moved = sum(a.size * a.dtype.itemsize for a in args)
    if space is HBM:
        args = [pltpu.with_memory_space_constraint(a, pltpu.HBM) for a in args]
    return pl.pallas_call(
        kernel,
        out_shape=[jax.ShapeDtypeStruct(shape, kind) for shape, kind in outs],
        in_specs=[SMEM] * len(scalars) + spaces,
        out_specs=out_spaces,
        input_output_aliases=aliases,
        scratch_shapes=scratch,
        compiler_params=pltpu.CompilerParams(vmem_limit_bytes=40 * 2**20),
        cost_estimate=pl.CostEstimate(flops=flops, bytes_accessed=moved, transcendentals=0),
    )(*scalars, *args)


def on_device(inputs, ln_gain, query_weight, out_weight, kv_cache, new_kv, active_heads):
    tensor_size = lax.axis_size("tensor")
    pipe_size = lax.axis_size("pipe")
    chips = tensor_size // 2
    section = lax.axis_index("pipe")
    slot = lax.axis_index("tensor")
    rows, positions, model = inputs.shape
    width = model // tensor_size
    tokens = rows * positions
    inner = query_weight.shape[2]
    heads = inner // HEAD_DIM
    past = kv_cache.shape[3]
    swap = [(i, i ^ 1) for i in range(tensor_size)]
    place = jnp.stack([section, slot // 2, slot % 2, slot * heads, chips]).astype(jnp.int32)

    def across(value):
        return lax.ppermute(value, "tensor", swap)

    def send(value, by, stages):
        pairs = []
        for stage in range(pipe_size):
            for at in range(tensor_size):
                target = (stage + stages) % pipe_size * tensor_size + (at + 2 * by) % tensor_size
                pairs.append((stage * tensor_size + at, target))
        return lax.ppermute(value, ("pipe", "tensor"), pairs)

    half, full = jnp.bfloat16, jnp.float32
    chunk = ((tokens, width), half)
    kept_chunk = ((tokens, width), full)
    last_outs = [chunk, kept_chunk]
    kept, given, current, query_w, cache, fresh, keep_w, give_w = call(
        opening_kernel,
        (place,),
        active_heads,
        inputs,
        ln_gain,
        query_weight,
        kv_cache,
        new_kv,
        out_weight,
        space=HBM,
        outs=[
            ((tokens, chips * width), full),
            ((tokens, chips * width), half),
            chunk,
            ((model, inner), half),
            ((2, rows, past, inner), half),
            ((2, tokens, inner), half),
            ((inner, chips * width), half),
            ((inner, chips * width), half),
        ],
        scratch=[
            pltpu.SMEM(active_heads.shape, jnp.int32),
            pltpu.VMEM((rows, positions, model), half),
            pltpu.VMEM((1, model), full),
            pltpu.VMEM((2, rows, positions, inner), half),
            pltpu.SemaphoreType.DMA((17 + 2 * chips,)),
        ],
    )
    *sent, last_chunk, own_chunk, give_w = call(
        merge_kernel,
        (),
        kept,
        across(given),
        current,
        give_w,
        outs=[chunk, chunk, chunk, kept_chunk, ((inner, chips * width), half)],
        passed=True,
    )
    last = [last_chunk, own_chunk]
    take_w = across(give_w)
    result = None
    for step in range(pipe_size):
        if step > 0:
            hopped = send(updated, 0, 1)
            arrived = {0: hopped, **{index: send(hopped, index, 0) for index in ORDER[:3]}}
            current = arrived[0]
            blocks = [b for i in ARRIVALS for b in (arrived[i], across(arrived[i]))]
            [attended] = call(
                functools.partial(layer_kernel, positions),
                (place, active_heads),
                *blocks,
                ln_gain,
                query_w,
                cache,
                fresh,
                outs=[((tokens, inner), half)],
            )
            other = across(attended)
            factors = (attended, other, keep_w, take_w)
            sent = call(project_kernel, (), *factors, outs=[chunk, chunk])
            last = call(project_kernel, (), *factors, current, outs=last_outs)
        summed = last[1]
        for index, part in zip(ORDER, (*sent, last[0])):
            summed = summed + send(part, index, 0).astype(full)
        updated = summed.astype(half)
        result = updated if result is None else jnp.where(section == step, updated, result)
    return result.reshape(1, rows, positions, width)


def solution(mesh):
    return jax.shard_map(
        on_device,
        mesh=mesh,
        in_specs=(
            P("dp", None, None),
            P("pipe", None),
            P("pipe", None, "tensor"),
            P("pipe", "tensor", None),
            P("pipe", None, "dp", None, "tensor"),
            P("pipe", None, "dp", None, "tensor"),
            P("dp", None, None),
        ),
        out_specs=P("pipe", "dp", None, "tensor"),
        check_vma=False,
    )
```

```python
import functools

import jax
import jax.numpy as jnp
from jax import lax
from jax.experimental import pallas as pl
from jax.experimental.pallas import tpu as pltpu
from jax.sharding import PartitionSpec as P

HEAD_DIM = 128
MB_ROWS = 8
NEGATIVE = -1e30
EPSILON = 1e-05
SCALE = HEAD_DIM ** (-0.5)
ORDER = (2, 1, 3, 0)
ARRIVALS = (0, 2, 1, 3)
GROUP_ROWS = 4
PASSED = 4


def normed_queries(blocks, gains, weights):
    tokens = blocks[0].shape[0]
    model = sum(block.shape[1] for block in blocks)
    total = jnp.zeros((tokens, 1), jnp.float32)
    for block in blocks:
        total += jnp.sum(block, axis=1, keepdims=True)
    centre = total / model
    total = jnp.zeros((tokens, 1), jnp.float32)
    for block in blocks:
        total += jnp.sum(jnp.square(block - centre), axis=1, keepdims=True)
    scale = lax.rsqrt(total / model + EPSILON)
    queries = [0.0] * len(weights[0]())
    for block, gain, weight in zip(blocks, gains, weights):
        normed = ((block - centre) * scale * gain).astype(jnp.bfloat16)
        for at, matrix in enumerate(weight()):
            queries[at] += jnp.dot(normed, matrix, preferred_element_type=jnp.float32)
    return [(query * SCALE).astype(jnp.bfloat16) for query in queries]


def attention(section, name_base, first_micro, active, queries, cache, fresh, positions):
    tokens = queries.shape[0]
    heads = queries.shape[1] // HEAD_DIM
    past = cache.shape[2]
    group = GROUP_ROWS * positions
    row_at = lax.broadcasted_iota(jnp.int32, (group, GROUP_ROWS * past), 0)
    column_at = lax.broadcasted_iota(jnp.int32, (group, GROUP_ROWS * past), 1)
    cached_mask = row_at // positions == column_at // past
    row_at = lax.broadcasted_iota(jnp.int32, (tokens, tokens), 0)
    column_at = lax.broadcasted_iota(jnp.int32, (tokens, tokens), 1)
    own_mask = (row_at // positions == column_at // positions) & (column_at <= row_at)
    transposed = (((1,), (1,)), ((), ()))
    groups = [
        (slice(at * GROUP_ROWS, (at + 1) * GROUP_ROWS), slice(at * group, (at + 1) * group))
        for at in range(tokens // group)
    ]
    lanes = [slice(head * HEAD_DIM, (head + 1) * HEAD_DIM) for head in range(heads)]
    scores = []
    for lane in lanes:
        own = lax.dot_general(
            queries[:, lane], fresh[0, :, lane], transposed, preferred_element_type=jnp.float32
        )
        cached = []
        for rows, here in groups:
            keys = cache[0, rows, :, lane].reshape(GROUP_ROWS * past, HEAD_DIM)
            score = lax.dot_general(
                queries[here, lane], keys, transposed, preferred_element_type=jnp.float32
            )
            cached.append(jnp.where(cached_mask, score, NEGATIVE))
        scores.append((jnp.where(own_mask, own, NEGATIVE), cached))
    weights = []
    for own, cached in scores:
        own_weights, cached_weights = [], []
        for score, (_, here) in zip(cached, groups):
            new = own[here]
            top = jnp.maximum(
                jnp.max(score, axis=1, keepdims=True), jnp.max(new, axis=1, keepdims=True)
            )
            score = jnp.exp(score - top)
            new = jnp.exp(new - top)
            share = 1.0 / (
                jnp.sum(score, axis=1, keepdims=True) + jnp.sum(new, axis=1, keepdims=True)
            )
            cached_weights.append((score * share).astype(jnp.bfloat16))
            own_weights.append((new * share).astype(jnp.bfloat16))
        weights.append((jnp.concatenate(own_weights, axis=0), cached_weights))
    result = []
    for head, (lane, (own, cached)) in enumerate(zip(lanes, weights)):
        mixed = jnp.dot(own, fresh[1, :, lane], preferred_element_type=jnp.float32)
        parts = []
        for weight, (rows, here) in zip(cached, groups):
            values = cache[1, rows, :, lane].reshape(GROUP_ROWS * past, HEAD_DIM)
            part = mixed[here] + jnp.dot(weight, values, preferred_element_type=jnp.float32)
            micro = first_micro + rows.start // MB_ROWS
            active_now = active[micro, section, 0] == name_base + head
            for entry in range(1, active.shape[2]):
                active_now |= active[micro, section, entry] == name_base + head
            parts.append(jnp.where(active_now, part, 0.0).astype(jnp.bfloat16))
        result.append(jnp.concatenate(parts, axis=0))
    return jnp.concatenate(result, axis=1)


def opening_kernel(
    place, active_in, inputs, gain_in, query_w, cache, new, own_w,
    kept, given, own_block, query_out, own_out, keep_cache, give_cache, keep_fresh, give_fresh,
    active, held, gain, new_held, queries, sems,
):
    rows, positions, model = held.shape
    chip, core = place[1], place[2]
    half, inner = keep_fresh.shape[1:]
    half_rows = rows // 2
    width = own_block.shape[1]
    parts = 4
    depth = model // parts
    loads = [pltpu.make_async_copy(inputs, held, sems.at[0])]
    small = [
        pltpu.make_async_copy(gain_in, gain, sems.at[parts + 5]),
        pltpu.make_async_copy(active_in, active, sems.at[parts + 6]),
    ]
    for part in range(parts):
        span = pl.ds(part * depth, depth)
        loads.append(
            pltpu.make_async_copy(query_w.at[0, span, :], query_out.at[span, :], sems.at[1 + part])
        )
    loads.append(pltpu.make_async_copy(new.at[0], new_held, sems.at[parts + 1]))
    sides = ((core, keep_cache, keep_fresh), (1 - core, give_cache, give_fresh))
    for at, (side, to, _) in enumerate(sides):
        taken = pl.ds(side * half_rows, half_rows)
        loads.append(pltpu.make_async_copy(cache.at[0, :, taken], to, sems.at[parts + 2 + at]))
    loads.append(pltpu.make_async_copy(own_w.at[0], own_out, sems.at[parts + 4]))
    for load in small + loads:
        load.start()
    loads[0].wait()
    small[0].wait()
    blocks, gains, weights = [], [], []
    waited = []
    for part in range(parts):
        span = slice(part * depth, (part + 1) * depth)
        blocks.append(held[:, :, span].reshape(2 * half, depth).astype(jnp.float32))
        gains.append(gain[:, span])

        def weight(part=part, span=span):
            if part not in waited:
                waited.append(part)
                loads[1 + part].wait()
            return [query_out[span, :]]

        weights.append(weight)
    start = pl.multiple_of(chip * width, 128)
    mine = pl.ds(core * half_rows, half_rows)
    own_block[...] = held[mine, :, pl.ds(start, width)].reshape(half, width)
    queries[...] = normed_queries(blocks, gains, weights)[0]
    loads[parts + 1].wait()
    for side, _, to in sides:
        taken = pl.ds(side * half_rows, half_rows)
        for part in range(2):
            to[part] = new_held[part, taken].reshape(half, inner)
    small[1].wait()
    attended = []
    for at, (side, some_cache, some_fresh) in enumerate(sides):
        loads[parts + 2 + at].wait()
        query = queries[pl.ds(pl.multiple_of(side * half, half), half), :]
        first = side * (half_rows // MB_ROWS)
        attended.append(
            attention(place[0], place[3], first, active, query, some_cache, some_fresh, positions)
        )
    loads[parts + 4].wait()
    attended = jnp.concatenate(attended, axis=0)
    for at, index in enumerate(ORDER):
        target = lax.rem(chip + index, place[4])
        columns = pl.ds(pl.multiple_of(target * width, 128), width)
        to = slice(at * width, (at + 1) * width)
        result = jnp.dot(attended, own_out[:, columns], preferred_element_type=jnp.float32)
        kept[:, to] = result[:half]
        given[:, to] = result[half:].astype(given.dtype)


def merge_kernel(kept, taken, current, *refs):
    outs = refs[PASSED : PASSED + len(ORDER)]
    width = current.shape[1]
    for at, out in enumerate(outs):
        here = slice(at * width, (at + 1) * width)
        part = kept[:, here] + taken[:, here].astype(jnp.float32)
        if at == len(ORDER) - 1:
            part += current[...].astype(jnp.float32)
        out[...] = part.astype(out.dtype)


def layer_kernel(positions, place, active, *refs):
    blocks = refs[: len(ARRIVALS)]
    gain = refs[len(ARRIVALS)]
    query_ws, out_ws, caches, fresh = (refs[at : at + 2] for at in range(len(ARRIVALS) + 1, 13, 2))
    outs = refs[13:]
    section, chip, core, base, chips = (place[at] for at in range(5))
    tokens, width = blocks[0].shape
    inner = query_ws[0].shape[1]
    heads = inner // HEAD_DIM
    first = core * (tokens // positions // MB_ROWS)
    values, gains, weights = [], [], []
    for index, block in zip(ARRIVALS, blocks):
        source = lax.rem(chip + chips - index, chips)
        span = pl.ds(pl.multiple_of(source * width, 128), width)
        values.append(block[...].astype(jnp.float32))
        gains.append(gain[:, span])
        weights.append(lambda span=span: [matrix[span, :] for matrix in query_ws])
    queries = normed_queries(values, gains, weights)
    bases = (base, base + heads * (1 - 2 * core))
    attended = [
        attention(section, bases[at], first, active, queries[at], caches[at], fresh[at], positions)
        for at in range(2)
    ]
    for at, index in enumerate(ORDER):
        target = lax.rem(chip + index, chips)
        columns = pl.ds(pl.multiple_of(target * width, 128), width)
        result = jnp.dot(attended[0], out_ws[0][:, columns], preferred_element_type=jnp.float32)
        result += jnp.dot(attended[1], out_ws[1][:, columns], preferred_element_type=jnp.float32)
        if at == len(ORDER) - 1:
            result += blocks[0][...].astype(jnp.float32)
        outs[at][...] = result.astype(outs[at].dtype)


VMEM = pl.BlockSpec(memory_space=pltpu.VMEM)
SMEM = pl.BlockSpec(memory_space=pltpu.SMEM)
HBM = pl.BlockSpec(memory_space=pltpu.HBM)


def call(kernel, scalars, *args, outs, space=VMEM, scratch=(), flops=0, passed=False):
    spaces = [space] * len(args)
    out_spaces = [VMEM] * len(outs)
    aliases = {}
    if passed:
        for at in range(PASSED):
            spaces[len(args) - 1 - at] = pl.BlockSpec(memory_space=pl.ANY)
            out_spaces[len(outs) - 1 - at] = pl.BlockSpec(memory_space=pl.ANY)
            aliases[len(scalars) + len(args) - 1 - at] = len(outs) - 1 - at
    moved = sum(a.size * a.dtype.itemsize for a in args)
    if space is HBM:
        args = [pltpu.with_memory_space_constraint(a, pltpu.HBM) for a in args]
    return pl.pallas_call(
        kernel,
        out_shape=[jax.ShapeDtypeStruct(shape, kind) for shape, kind in outs],
        in_specs=[SMEM] * len(scalars) + spaces,
        out_specs=out_spaces,
        input_output_aliases=aliases,
        scratch_shapes=scratch,
        compiler_params=pltpu.CompilerParams(vmem_limit_bytes=24 * 2**20),
        cost_estimate=pl.CostEstimate(flops=flops, bytes_accessed=moved, transcendentals=0),
    )(*scalars, *args)


def on_device(inputs, ln_gain, query_weight, out_weight, kv_cache, new_kv, active_heads):
    tensor_size = lax.axis_size("tensor")
    pipe_size = lax.axis_size("pipe")
    chips = tensor_size // 2
    section = lax.axis_index("pipe")
    slot = lax.axis_index("tensor")
    rows, positions, model = inputs.shape
    width = model // tensor_size
    tokens = rows * positions
    inner = query_weight.shape[2]
    heads = inner // HEAD_DIM
    past = kv_cache.shape[3]
    swap = [(i, i ^ 1) for i in range(tensor_size)]
    place = jnp.stack([section, slot // 2, slot % 2, slot * heads, chips]).astype(jnp.int32)

    def across(value):
        return lax.ppermute(value, "tensor", swap)

    def send(value, by, stages):
        pairs = []
        for stage in range(pipe_size):
            for at in range(tensor_size):
                target = (stage + stages) % pipe_size * tensor_size + (at + 2 * by) % tensor_size
                pairs.append((stage * tensor_size + at, target))
        return lax.ppermute(value, ("pipe", "tensor"), pairs)

    half, full = jnp.bfloat16, jnp.float32
    count, wide = tokens // 2, model // chips
    chunks = [((count, wide), half)] * (chips - 1) + [((count, wide), full)]
    passed = [
        ((model, inner), half),
        ((inner, model), half),
        ((2, rows // 2, past, inner), half),
        ((2, count, inner), half),
    ]
    kept, given, current, query_w, out_w, keep_cache, give_cache, keep_fresh, give_fresh = call(
        opening_kernel,
        (place,),
        active_heads,
        inputs,
        ln_gain,
        query_weight,
        kv_cache,
        new_kv,
        out_weight,
        space=HBM,
        outs=[
            ((count, model), full),
            ((count, model), half),
            ((count, wide), half),
            *passed[:2],
            *passed[2:3] * 2,
            *passed[3:] * 2,
        ],
        scratch=[
            pltpu.SMEM(active_heads.shape, jnp.int32),
            pltpu.VMEM((rows, positions, model), half),
            pltpu.VMEM((1, model), full),
            pltpu.VMEM((2, rows, positions, inner), half),
            pltpu.VMEM((tokens, inner), half),
            pltpu.SemaphoreType.DMA((11,)),
        ],
    )
    *parts, query_w, out_w, give_cache, give_fresh = call(
        merge_kernel,
        (),
        kept,
        across(given),
        current,
        query_w,
        out_w,
        give_cache,
        give_fresh,
        outs=[*chunks, *passed],
        passed=True,
    )
    query_ws = (query_w, across(query_w))
    out_ws = (out_w, across(out_w))
    caches = (keep_cache, across(give_cache))
    fresh = (keep_fresh, across(give_fresh))
    result = None
    for step in range(pipe_size):
        if step > 0:
            hopped = send(updated, 0, 1)
            blocks = [hopped, *(send(hopped, index, 0) for index in ARRIVALS[1:])]
            parts = call(
                functools.partial(layer_kernel, positions),
                (place, active_heads),
                *blocks,
                ln_gain,
                *query_ws,
                *out_ws,
                *caches,
                *fresh,
                outs=chunks,
            )
        summed = parts[-1]
        for index, part in zip(ORDER, parts[:-1]):
            summed = summed + send(part, index, 0).astype(full)
        updated = summed.astype(half)
        result = updated if result is None else jnp.where(section == step, updated, result)
    left, right = result[:, :width], result[:, width:]
    odd = slot % 2 == 1
    own = jnp.where(odd, right, left)
    taken = across(jnp.where(odd, left, right))
    first, second = jnp.where(odd, taken, own), jnp.where(odd, own, taken)
    return jnp.concatenate([first, second], axis=0).reshape(1, rows, positions, width)


def solution(mesh):
    return jax.shard_map(
        on_device,
        mesh=mesh,
        in_specs=(
            P("dp", None, None),
            P("pipe", None),
            P("pipe", None, "tensor"),
            P("pipe", "tensor", None),
            P("pipe", None, "dp", None, "tensor"),
            P("pipe", None, "dp", None, "tensor"),
            P("dp", None, None),
        ),
        out_specs=P("pipe", "dp", None, "tensor"),
        check_vma=False,
    )
```
